256 devices in a mesh: body: 64 (over y, z, core), across: 4 (over x).
Axes of the slice: x: 4, y: 4, z: 8, core: 2. Of those that a mesh axis runs over, the one named last changes fastest.
Arguments:
- cotangent: float32 [3, 512, 128, 256], P(None, 'body', 'across'), may hold values from -6 to 6
- shear_modulus: float32 [512, 128, 256], P('body', 'across'), may hold values from 0.3 to 3
- lame_first: float32 [512, 128, 256], P('body', 'across'), may hold values from 0.3 to 3
- inertia: float32 [512, 128, 256], P('body', 'across'), may hold values from 0.02 to 0.2
- surface_points: float32 [64, 4, 16, 3, 128], P('body', 'across'), may hold values from -0.3 to 1, as said below
- point_counts: int32 [64, 4, 16], P('body', 'across'), may hold values from 64 to 128, as said below
- surface_maps: int32 [64, 4, 16, 128], P('body', 'across'), may hold values from 0 to 65535, as said below
- contact_pairs: int32 [64, 4, 3, 256], P('body', 'across'), may hold values from 0 to 63, as said below
Outputs:
- displacement: float32 [3, 512, 128, 256], P(None, 'body', 'across')
- residual: float32 [3, 512, 128, 256], P(None, 'body', 'across')
The draws below stay inside these ranges and needn't reach their ends.
Inputs may be any that keep to these rules, and one draw needn't show every extreme that they name: `surface_points`: coordinates 0 and 1 lie in [0, 1]; coordinate 2 lies in [0.3, 0.6] for even-numbered blocks and in [-0.3, 0] for odd-numbered blocks. `point_counts`: every device has a block with all 128 points active. `surface_maps`: the cells of one device's points are distinct. `contact_pairs`: row 0 holds even block numbers and row 2 odd block numbers below 16; row 1 is a first-split index, and the partner shares the device's second-split index. Every device names every first-split index, its own included, exactly 4 times.
All inputs are finite; a program needn't handle non-finite values.
Results may differ from the reference program's by a relative error of at most 0.0003.
Values sent between devices are 32-bit elements; how exact they have to be, the bound alone decides.
A program may use at most 192 MiB of HBM per device.

```python
import math
import jax
import jax.numpy as jnp
from jax import lax

SX = 8
SY = 32
SZ = 256
PTS = 128
BLK_DEV = 16
CAP = 4
ITERS = 2
SLABS = 64
ACROSS = 4
FINGER_SLABS = 16
PAIR_DEV = 256
NX = 512
NY = 128
NZ = 256
CELLS = 65536


def draw_surface_points(key, part):
    key_list = jax.random.split(key, 2)
    planar = jax.random.uniform(key_list[0], (SLABS, ACROSS, BLK_DEV, 2, PTS), jnp.float32)
    height_draw = jax.random.uniform(key_list[1], (SLABS, ACROSS, BLK_DEV, 1, PTS), jnp.float32)
    upper = (jnp.arange(BLK_DEV) % 2 == 0)[None, None, :, None, None]
    height = jnp.where(upper, 0.3 + 0.3 * height_draw, -0.3 * height_draw)
    return jnp.concatenate([planar, height], axis=3).astype(jnp.float32)


def draw_point_counts(key, part):
    counts = jax.random.randint(key, (SLABS, ACROSS, BLK_DEV), PTS // 2, PTS + 1, dtype=jnp.int32)
    counts = counts.at[:, :, 0].set(PTS)
    counts = counts.at[:, :, 1].set(PTS // 2)
    return counts


def draw_surface_maps(key, part):

    def one_device(device_index):
        device_key = jax.random.fold_in(key, device_index)
        key_list = jax.random.split(device_key, 2)
        inner_cells = jax.random.permutation(key_list[0], CELLS - 2)[:BLK_DEV * PTS - 2] + 1
        chosen = jnp.concatenate([jnp.array([0, CELLS - 1], dtype=jnp.int32), inner_cells.astype(jnp.int32)])
        return jax.random.permutation(key_list[1], chosen).reshape(BLK_DEV, PTS).astype(jnp.int32)
    return jax.vmap(one_device)(jnp.arange(SLABS * ACROSS, dtype=jnp.int32)).reshape(SLABS, ACROSS, BLK_DEV, PTS)


def draw_contact_pairs(key, part):

    def one_device(device_index):
        device_key = jax.random.fold_in(key, device_index)
        key_list = jax.random.split(device_key, 3)
        partner_rows = (jax.random.permutation(key_list[0], PAIR_DEV) // CAP).astype(jnp.int32)
        own_blocks = 2 * jax.random.randint(key_list[1], (PAIR_DEV,), 0, BLK_DEV // 2, dtype=jnp.int32)
        partner_blocks = 2 * jax.random.randint(key_list[2], (PAIR_DEV,), 0, BLK_DEV // 2, dtype=jnp.int32) + 1
        own_blocks = own_blocks.at[0].set(0)
        partner_blocks = partner_blocks.at[0].set(BLK_DEV - 1)
        return jnp.stack([own_blocks, partner_rows, partner_blocks]).astype(jnp.int32)
    return jax.vmap(one_device)(jnp.arange(SLABS * ACROSS, dtype=jnp.int32)).reshape(SLABS, ACROSS, 3, PAIR_DEV)


def shard_levels(key, extent, shards, smallest, largest):
    loudness, own = 1.0, jax.random.fold_in(key, 6)
    for axis_at, shards_of in shards:
        draws = jnp.exp(jax.random.uniform(jax.random.fold_in(own, axis_at), (shards_of,), jnp.float32, smallest / len(shards), largest / len(shards)))
        loudness = loudness * jnp.repeat(draws, extent[axis_at] // shards_of).reshape([-1 if axis == axis_at else 1 for axis in range(len(extent))])
    return loudness


def centred(rng, extent, width, bound, shards=(), kind=jnp.bfloat16):
    values = jax.random.normal(rng, extent, jnp.float32) * width
    if len(shards) > 0:
        values = shard_levels(rng, extent, shards, -0.22, 0.18) * values
    return jnp.clip(values, min=-bound, max=bound).astype(kind)


def setup_inputs(seed: int = 0) -> dict:
    keys = jax.random.split(jax.random.key(seed), 9)
    cotangent = centred(keys[0], (3, NX, NY, NZ), 1.0, 6.0, ((1, 64), (2, 4)), jnp.float32)
    shear_modulus = jnp.clip(jnp.exp(math.log(3.0) - 2.3025851 * jax.random.uniform(keys[1], (NX, NY, NZ), jnp.float32) ** shard_levels(keys[1], (NX, NY, NZ), ((0, 64), (1, 4)), -0.2, 0.2)), 0.3, 3.0)
    lame_first = jnp.clip(jnp.exp(math.log(3.0) - 2.3025851 * jax.random.uniform(keys[2], (NX, NY, NZ), jnp.float32) ** shard_levels(keys[2], (NX, NY, NZ), ((0, 64), (1, 4)), -0.2, 0.2)), 0.3, 3.0)
    inertia = jnp.clip(jnp.exp(math.log(0.2) - 2.3025851 * jax.random.uniform(keys[3], (NX, NY, NZ), jnp.float32) ** shard_levels(keys[3], (NX, NY, NZ), ((0, 64), (1, 4)), -0.2, 0.2)), 0.02, 0.2)
    surface_points = draw_surface_points(jax.random.fold_in(keys[8], 71), 0)
    point_counts = draw_point_counts(jax.random.fold_in(keys[8], 71), 0)
    surface_maps = draw_surface_maps(jax.random.fold_in(keys[8], 71), 0)
    contact_pairs = draw_contact_pairs(jax.random.fold_in(keys[8], 71), 0)
    return dict(cotangent=cotangent, shear_modulus=shear_modulus, lame_first=lame_first, inertia=inertia, surface_points=surface_points, point_counts=point_counts, surface_maps=surface_maps, contact_pairs=contact_pairs)


barrier_reach = 1.0
barrier_scale = 0.005


def shifted(padded, direction, offset):
    leading = padded.ndim - 3
    selection = [slice(None)] * leading + [slice(1, -1)] * 3
    length = padded.shape[leading + direction]
    selection[leading + direction] = slice(1 + offset, length - 1 + offset)
    return padded[tuple(selection)]


def stencil_apply(vector, padded_vector, shear, lame, padded_shear, padded_lame, inertia, global_rows, cut_row):
    result = inertia[None] * vector
    for direction in range(3):
        selector = (jnp.arange(3) == direction).astype(jnp.float32)[:, None, None, None]
        stiffness = shear[None] + (lame + shear)[None] * selector
        for offset in (1, -1):
            near_vector = shifted(padded_vector, direction, offset)
            near_shear = shifted(padded_shear, direction, offset)
            near_lame = shifted(padded_lame, direction, offset)
            near_stiffness = near_shear[None] + (near_lame + near_shear)[None] * selector
            face_weight = 0.5 * (stiffness + near_stiffness)
            if direction == 0:
                blocked_row = cut_row - 1 if offset == 1 else cut_row
                keep_rows = jnp.where(global_rows == blocked_row, 0.0, 1.0).astype(jnp.float32)
                face_weight = face_weight * keep_rows[None, :, None, None]
            result = result + face_weight * (vector - near_vector)
    return result


def barrier_weights(first_points, second_points, first_count, second_count, live_flag):
    offsets = first_points[:, :, None] - second_points[:, None, :]
    squared = jnp.sum(offsets * offsets, axis=0)
    point_width = first_points.shape[1]
    point_ranks = jnp.arange(point_width, dtype=jnp.int32)
    active = (point_ranks[:, None] < first_count) & (point_ranks[None, :] < second_count)
    active = active & (squared < barrier_reach) & (live_flag > 0)
    safe = jnp.where(active, squared, barrier_reach)
    excess = safe - barrier_reach
    return barrier_scale * (-2.0 * jnp.log(safe / barrier_reach) - 4.0 * excess / safe + (excess * excess) / (safe * safe))


def pair_forces(weights, first_moves, second_moves):
    first_side = first_moves * jnp.sum(weights, axis=1)[None, :] - jnp.einsum("ij,cj->ci", weights, second_moves, precision=lax.Precision.HIGHEST)
    second_side = second_moves * jnp.sum(weights, axis=0)[None, :] - jnp.einsum("ij,ci->cj", weights, first_moves, precision=lax.Precision.HIGHEST)
    return first_side, second_side


def pair_task(packed):
    first_points, second_points, first_moves, second_moves, first_count, second_count, live_flag = packed
    weights = barrier_weights(first_points, second_points, first_count, second_count, live_flag)
    return pair_forces(weights, first_moves, second_moves)


def device_view(vector):
    return vector.reshape(3, SLABS, SX, ACROSS, SY, SZ).transpose(1, 3, 0, 2, 4, 5).reshape(SLABS, ACROSS, 3, SX * SY * SZ)


def grid_view(blocks):
    return blocks.reshape(SLABS, ACROSS, 3, SX, SY, SZ).transpose(2, 0, 3, 1, 4, 5).reshape(3, NX, NY, NZ)


def pick_points(values, cell_maps):
    return values[:, cell_maps].transpose(1, 0, 2)


def place_points(values, cell_maps, forces):
    return values.at[:, cell_maps].add(forces.transpose(1, 0, 2))


def contact(vector, surface_points, point_counts, surface_maps, contact_pairs):
    block_moves = jax.vmap(jax.vmap(pick_points))(device_view(vector), surface_maps)
    slab_ids = jnp.broadcast_to(jnp.arange(SLABS, dtype=jnp.int32)[:, None, None], (SLABS, ACROSS, PAIR_DEV)).reshape(-1)
    across_ids = jnp.broadcast_to(jnp.arange(ACROSS, dtype=jnp.int32)[None, :, None], (SLABS, ACROSS, PAIR_DEV)).reshape(-1)
    own_blocks = contact_pairs[:, :, 0, :].reshape(-1)
    partner_rows = contact_pairs[:, :, 1, :].reshape(-1)
    partner_blocks = contact_pairs[:, :, 2, :].reshape(-1)
    packed = (surface_points[slab_ids, across_ids, own_blocks],
              surface_points[partner_rows, across_ids, partner_blocks],
              block_moves[slab_ids, across_ids, own_blocks],
              block_moves[partner_rows, across_ids, partner_blocks],
              point_counts[slab_ids, across_ids, own_blocks],
              point_counts[partner_rows, across_ids, partner_blocks],
              jnp.ones_like(own_blocks))
    first_side, second_side = lax.map(pair_task, packed, batch_size=64)
    forces = jnp.zeros_like(block_moves).at[slab_ids, across_ids, own_blocks].add(first_side)
    forces = forces.at[partner_rows, across_ids, partner_blocks].add(second_side)
    spread = jax.vmap(jax.vmap(place_points))(jnp.zeros((SLABS, ACROSS, 3, SX * SY * SZ), jnp.float32), surface_maps, forces)
    return grid_view(spread)


def reference(cotangent, shear_modulus, lame_first, inertia, surface_points, point_counts, surface_maps, contact_pairs):
    padded_shear = jnp.pad(shear_modulus, 1)
    padded_lame = jnp.pad(lame_first, 1)
    global_rows = jnp.arange(NX, dtype=jnp.int32)
    cut_row = FINGER_SLABS * SX

    def apply_system(vector):
        padded_vector = jnp.pad(vector, ((0, 0), (1, 1), (1, 1), (1, 1)))
        elastic = stencil_apply(vector, padded_vector, shear_modulus, lame_first, padded_shear, padded_lame, inertia, global_rows, cut_row)
        return elastic + contact(vector, surface_points, point_counts, surface_maps, contact_pairs)

    displacement = jnp.zeros_like(cotangent)
    residual = cotangent
    direction = cotangent
    norm_now = jnp.sum(residual * residual)
    for iteration in range(ITERS):
        applied = apply_system(direction)
        step_length = norm_now / jnp.sum(direction * applied)
        displacement = displacement + step_length * direction
        residual = residual - step_length * applied
        norm_next = jnp.sum(residual * residual)
        direction = residual + (norm_next / norm_now) * direction
        norm_now = norm_next
    return displacement, residual
```

```python
import functools

import jax
import jax.numpy as jnp
from jax import lax
from jax.experimental import pallas as pl
from jax.experimental.pallas import tpu as pltpu
from jax.sharding import PartitionSpec as P

MESH = pl.DeviceIdType.MESH
CAP = 4
ROWS, COLS, DEPTH = 8, 32, 256
BLOCKS, WIDTH = 16, 128
MOVE = 3 * WIDTH
F32, BF16 = jnp.float32, jnp.bfloat16
FAR = 100.0


def iota(shape, dim):
    return lax.broadcasted_iota(jnp.int32, shape, dim)


def fiota(shape, dim):
    return iota(shape, dim).astype(F32)


def parts2(x):
    high = x.astype(BF16)
    return high, (x - high.astype(F32)).astype(BF16)


def parts3(x):
    high = x.astype(BF16).astype(F32)
    rest = x - high
    mid = rest.astype(BF16).astype(F32)
    return high, mid, rest - mid


def lanes_t(a, b):
    return lax.dot_general(a, b, (((1,), (1,)), ((), ())), preferred_element_type=F32)


def plain(a, b):
    return jnp.dot(a, b, preferred_element_type=F32)


def kernel(
    nb, na,
    c_hbm, mu_hbm, lam_hbm, inertia_hbm, pts_ref, cnt_ref, map_ref, pair_ref,
    disp_hbm, res_hbm,
    cx, qx, q2, mx, inertia, fw, ez, vh, vm, lhs, ws,
    moves0, moves1, mparts, pparts, ytab, ownc, tgtc, ownr, second, rowt, colt, forces,
    psend, pgot, msend, mgot, rsend, rgot, fsend, fgot, bsend, bgot,
    ysend, ygot, ysend1, ygot1, arsend, argot, outs,
    sem_in, sem_out, a2a_send, a2a_recv, halo_send, halo_recv, ar_send, ar_recv,
):
    b = lax.axis_index("body")
    a = lax.axis_index("across")
    slots = nb * CAP
    groups = nb // 2
    me_g = b // 2

    def wrap(i, n):
        return lax.rem(i + n, n)

    loads = [
        pltpu.make_async_copy(c_hbm, cx.at[:, pl.ds(1, ROWS)], sem_in.at[0]),
        pltpu.make_async_copy(mu_hbm, mx.at[0, pl.ds(1, ROWS)], sem_in.at[1]),
        pltpu.make_async_copy(lam_hbm, mx.at[1, pl.ds(1, ROWS)], sem_in.at[2]),
        pltpu.make_async_copy(inertia_hbm, inertia, sem_in.at[3]),
    ]
    for load in loads:
        load.start()

    table = pair_ref[...].astype(F32)
    own_row, partner_row, target_row = table[0:1], table[1:2], table[2:3]
    sub, lane = iota((slots, slots), 0), iota((slots, slots), 1)
    eye = sub == lane
    partner_col = jnp.sum(jnp.where(eye, partner_row, 0.0), axis=1, keepdims=True)
    rank = jnp.sum(
        jnp.where((partner_col == partner_row) & (sub < lane), 1.0, 0.0), axis=0, keepdims=True
    )
    slot_row = partner_row * CAP + rank
    chosen = slot_row == sub.astype(F32)
    own_col = jnp.sum(jnp.where(chosen, own_row, 0.0), axis=1, keepdims=True)
    target_col = jnp.sum(jnp.where(chosen, target_row, 0.0), axis=1, keepdims=True)
    ownc[...] = jnp.broadcast_to(own_col, (slots, WIDTH))
    tgtc[...] = jnp.broadcast_to(target_col, (slots, WIDTH))
    ownr[...] = jnp.sum(jnp.where(eye, own_col, 0.0), axis=0, keepdims=True)

    block_id = iota((BLOCKS, WIDTH), 0)
    count = jnp.zeros((BLOCKS, WIDTH), jnp.int32)
    for k in range(BLOCKS):
        count = jnp.where(block_id == k, cnt_ref[0, 0, k], count)
    active = iota((BLOCKS, WIDTH), 1) < count
    far = jnp.where(lax.rem(block_id, 2) == 0, FAR, -FAR)
    coords = [
        jnp.where(active, pts_ref[0, 0, :, 0, :] - 0.5, far),
        pts_ref[0, 0, :, 1, :] - 0.5,
        pts_ref[0, 0, :, 2, :],
    ]
    pad16 = jnp.zeros((BLOCKS, WIDTH), F32)

    def store_parts(ref, tiles):
        for c, tile in enumerate(tiles):
            stacked = jnp.concatenate([*parts3(tile)] + [pad16] * 5, axis=0)
            ref[:, c * WIDTH : (c + 1) * WIDTH] = stacked.astype(BF16)

    store_parts(pparts, coords)
    norm = coords[0] * coords[0] + coords[1] * coords[1] + coords[2] * coords[2]
    columns = [part for y in coords for part in parts3(-2.0 * y)] + [*parts3(norm)]
    for k, column in enumerate(columns):
        ytab[:, k * WIDTH : (k + 1) * WIDTH] = jnp.concatenate(
            [column] + [pad16] * 7, axis=0
        ).astype(BF16)

    lane8 = iota((8, WIDTH), 1)
    lane3 = jnp.where(lane8 < 3 * BLOCKS, lax.rem(lane8, BLOCKS), -1).astype(F32)
    lane1 = jnp.where(lane8 < BLOCKS, lane8, -1).astype(F32)
    sub8 = iota((8, WIDTH), 0)

    def select3(ids, ref):
        return plain(jnp.where(ids == lane3, 1.0, 0.0).astype(BF16), ref[...])

    def eight(ref, g):
        return jnp.concatenate([ref[2 * g], ref[2 * g + 1]], axis=0)

    def store_eight(ref, g, value):
        ref[2 * g] = value[:4]
        ref[2 * g + 1] = value[4:]

    def rows8(g):
        return pl.ds(pl.multiple_of(g * 8, 8), 8)

    def a2a(phase, src, dst, peer):
        return pltpu.make_async_remote_copy(
            src_ref=src.at[peer], dst_ref=dst.at[b],
            send_sem=a2a_send.at[phase, peer], recv_sem=a2a_recv.at[phase, b],
            device_id=(peer, a), device_id_type=MESH,
        )

    def arrival(phase, src, dst, peer):
        return pltpu.make_async_remote_copy(
            src_ref=src.at[peer], dst_ref=dst.at[peer],
            send_sem=a2a_send.at[phase, peer], recv_sem=a2a_recv.at[phase, peer],
            device_id=(peer, a), device_id_type=MESH,
        )

    def send_group(phase, src, dst, g):
        for h in range(2):
            peer = 2 * g + h

            @pl.when(peer != b)
            def _():
                a2a(phase, src, dst, peer).start()

            @pl.when(peer == b)
            def _():
                dst[peer] = src[peer]

    def wait_group(phase, src, dst, g):
        for h in range(2):
            peer = 2 * g + h

            @pl.when(peer != b)
            def _():
                arrival(phase, src, dst, peer).wait_recv()

    def each_group(body, sign):
        def step(t, carry):
            body(wrap(me_g + sign * t, groups))
            return carry

        lax.fori_loop(0, groups, step, 0)

    def points_out(g):
        at = rows8(g)
        value = jnp.concatenate([select3(ownc[at], pparts), tgtc[at]], axis=1)
        store_eight(psend, g, value)
        send_group(0, psend, pgot, g)

    each_group(points_out, 1)

    for load in loads:
        load.wait()
    up, down = wrap(b + 1, nb), wrap(b - 1, nb)
    right, left = wrap(a + 1, na), wrap(a - 1, na)

    def halo(k, src, dst, peer):
        return pltpu.make_async_remote_copy(
            src_ref=src, dst_ref=dst, send_sem=halo_send.at[k], recv_sem=halo_recv.at[k],
            device_id=peer, device_id_type=MESH,
        )

    last = ROWS
    for c in range(3):
        ysend[0, c] = cx[c, 1 : ROWS + 1, COLS - 1, :]
        ysend[1, c] = cx[c, 1 : ROWS + 1, 0, :]
    for m in range(2):
        ysend[0, 3 + m] = mx[m, 1 : ROWS + 1, COLS - 1, :]
        ysend[1, 3 + m] = mx[m, 1 : ROWS + 1, 0, :]
    halos0 = [
        halo(0, cx.at[:, last], cx.at[:, 0], (up, a)),
        halo(1, cx.at[:, 1], cx.at[:, last + 1], (down, a)),
        halo(2, mx.at[:, last], mx.at[:, 0], (up, a)),
        halo(3, mx.at[:, 1], mx.at[:, last + 1], (down, a)),
        halo(4, ysend.at[0], ygot.at[0], (b, right)),
        halo(5, ysend.at[1], ygot.at[1], (b, left)),
    ]
    for copy in halos0:
        copy.start()

    def place(k, carry):
        z = lax.rem(map_ref[0, 0, pl.ds(k, 1), :], DEPTH)
        ez[k] = jnp.where(iota((DEPTH, WIDTH), 0) == z, 1.0, 0.0).astype(BF16)
        return carry

    lax.fori_loop(0, BLOCKS, place, 0)

    def pick(vector, base, moves):
        for c in range(3):
            flat = vector[c, base : base + ROWS].reshape(ROWS * COLS, DEPTH)
            at = slice(c * 256, (c + 1) * 256)
            vh[at], vm[at] = parts2(flat)

        def step(k, rows):
            picked = plain(vh[...], ez[k]) + plain(vm[...], ez[k])
            xy = map_ref[0, 0, pl.ds(k, 1), :] // DEPTH
            mask = iota((256, WIDTH), 0) == xy
            made = []
            for c in range(3):
                kept = jnp.where(mask, picked[c * 256 : (c + 1) * 256], 0.0)
                row = jnp.sum(kept, axis=0, keepdims=True)
                made.append(jnp.where(block_id == k, row, rows[c]))
            return tuple(made)

        rows = lax.fori_loop(0, BLOCKS, step, (pad16,) * 3)
        moves[...] = jnp.concatenate(rows, axis=1)

    pick(cx, 1, moves0)

    def tiles(value):
        return [value[:, c * WIDTH : (c + 1) * WIDTH] for c in range(3)]

    def moves_out(phase, moves, src, dst):
        store_parts(mparts, tiles(moves[...]))

        def body(g):
            store_eight(src, g, select3(ownc[rows8(g)], mparts))
            send_group(phase, src, dst, g)

        each_group(body, 1)

    moves_out(1, moves0, msend, mgot)

    row32, lane256 = iota((COLS, DEPTH), 0), iota((COLS, DEPTH), 1)

    def clear_edges(xs, yhalo):
        @pl.when(b == 0)
        def _():
            for x in xs:
                x[:, 0] = jnp.zeros_like(x[:, 0])

        @pl.when(b == nb - 1)
        def _():
            for x in xs:
                x[:, last + 1] = jnp.zeros_like(x[:, last + 1])

        @pl.when(a == 0)
        def _():
            yhalo[0] = jnp.zeros_like(yhalo[0])

        @pl.when(a == na - 1)
        def _():
            yhalo[1] = jnp.zeros_like(yhalo[1])

    def beside(v, low, high):
        return (
            jnp.where(row32 == COLS - 1, high, pltpu.roll(v, COLS - 1, 0)),
            jnp.where(row32 == 0, low, pltpu.roll(v, 1, 0)),
            jnp.where(lane256 == DEPTH - 1, 0.0, pltpu.roll(v, DEPTH - 1, 1)),
            jnp.where(lane256 == 0, 0.0, pltpu.roll(v, 1, 1)),
        )

    def faces(i, carry):
        mu, lam = mx[0, i + 1], mx[1, i + 1]
        near_mu = (mx[0, i + 2], mx[0, i]) + beside(
            mu, ygot[0, 3, pl.ds(i, 1), :], ygot[1, 3, pl.ds(i, 1), :]
        )
        near_lam = (mx[1, i + 2], mx[1, i]) + beside(
            lam, ygot[0, 4, pl.ds(i, 1), :], ygot[1, 4, pl.ds(i, 1), :]
        )
        cut = nb // 4
        open_high = jnp.where((b == cut - 1) & (i == ROWS - 1), 0.0, 0.5)
        open_low = jnp.where((b == cut) & (i == 0), 0.0, 0.5)
        for k in range(6):
            half = (open_high, open_low, 0.5, 0.5, 0.5, 0.5)[k]
            plain_weight = half * (mu + near_mu[k])
            fw[k, 0, i] = plain_weight
            fw[k, 1, i] = 2.0 * plain_weight + half * (lam + near_lam[k])
        return carry

    def elastic(vector, yhalo, out, base, others):
        def plane(i, sums):
            sums = list(sums)
            for c in range(3):
                v = vector[c, i + 1]
                near = (vector[c, i + 2], vector[c, i]) + beside(
                    v, yhalo[0, c, pl.ds(i, 1), :], yhalo[1, c, pl.ds(i, 1), :]
                )
                value = inertia[i] * v
                for k in range(6):
                    value = value + fw[k, int(k // 2 == c), i] * (v - near[k])
                out[c, base + i] = value
                for n, other in enumerate(others):
                    sums[n] = sums[n] + value * other[c, i + 1]
            return tuple(sums)

        zero = jnp.zeros((COLS, DEPTH), F32)
        return lax.fori_loop(0, ROWS, plane, (zero,) * len(others))

    for copy in halos0:
        copy.wait_recv()
    clear_edges((cx, mx), ygot)
    lax.fori_loop(0, ROWS, faces, 0)
    (c_ec,) = elastic(cx, ygot, qx, 1, (cx,))
    pick(qx, 1, moves1)

    ones8 = jnp.ones((8, WIDTH), F32)

    def weigh(g):
        wait_group(0, psend, pgot, g)
        got = eight(pgot, g)
        ids = got[:, MOVE:]
        ys = plain(jnp.where(ids == lane1, 1.0, 0.0).astype(BF16), ytab[...])
        y = [ys[:, k * WIDTH : (k + 1) * WIDTH] for k in range(12)]
        xs = tiles(got)
        firsts, seconds = [], []
        for c in range(3):
            xh, xm, xl = parts3(xs[c])
            yh, ym, yl = y[3 * c : 3 * c + 3]
            firsts += [xh, xh, xm, xm, xh, xl]
            seconds += [yh, ym, yh, ym, yl, yh]
        norm = xs[0] * xs[0] + xs[1] * xs[1] + xs[2] * xs[2]
        firsts += [*parts3(norm), ones8, ones8, ones8]
        seconds += [ones8, ones8, ones8, *y[9:]]
        zero8 = jnp.zeros((8, WIDTH), F32)
        left_side = jnp.concatenate(firsts + [zero8] * 8, axis=0).T.astype(BF16)
        for r in range(8):
            right_side = jnp.concatenate(
                [jnp.where(sub8 == r, s, 0.0) for s in seconds] + [zero8] * 8, axis=0
            ).astype(BF16)
            squared = jnp.minimum(plain(left_side, right_side), 1.0)
            inverse = 1.0 / squared
            weight = 0.005 * (inverse * (inverse + 2.0) - 3.0) - 0.01 * jnp.log(squared)
            high, low = parts2(weight)
            ws[g * 8 + r, 0:WIDTH] = high
            ws[g * 8 + r, WIDTH : 2 * WIDTH] = low

    def stack(value, extra):
        rows = []
        for tile in tiles(value):
            high = tile.astype(BF16).astype(F32)
            rows += [high, tile - high]
        return jnp.concatenate(rows + extra, axis=0).astype(BF16)

    def sides(g, src, dst, first_phase):
        got = eight(dst, g)
        mine = select3(pgot_ids(g), mparts)
        extra = [ones8, ones8] if first_phase else []
        v_rows, u_rows = stack(got, extra), stack(mine, extra)
        v_rows = jnp.concatenate([v_rows, v_rows], axis=1)
        count = 4 if first_phase else 3
        into_second = [jnp.zeros((8, WIDTH), F32)] * count
        into_first = [jnp.zeros((8, WIDTH), F32)] * count
        for r in range(8):
            w = ws[g * 8 + r]
            to_second = plain(v_rows, w)
            to_first = lanes_t(u_rows, w)
            to_first = to_first[:, :WIDTH] + to_first[:, WIDTH:]
            for k in range(count):
                high, low = slice(16 * k, 16 * k + 8), slice(16 * k + 8, 16 * k + 16)
                if k < 3:
                    s, f = to_second[high] + to_second[low], to_first[high] + to_first[low]
                else:
                    s, f = to_second[high], to_first[high]
                into_second[k] = jnp.where(sub8 == r, s, into_second[k])
                into_first[k] = jnp.where(sub8 == r, f, into_first[k])
        at = rows8(g)
        if first_phase:
            rowt[at], colt[at] = into_first[3], into_second[3]
        row_total, col_total = rowt[at], colt[at]
        second[at] = jnp.concatenate(
            [u * col_total - s for u, s in zip(tiles(mine), into_second)], axis=1
        )
        return jnp.concatenate(
            [v * row_total - f for v, f in zip(tiles(got), into_first)], axis=1
        )

    def pgot_ids(g):
        return jnp.concatenate([pgot[2 * g, :, MOVE:], pgot[2 * g + 1, :, MOVE:]], axis=0)

    def group0(g):
        weigh(g)
        wait_group(1, msend, mgot, g)
        store_eight(rsend, g, sides(g, msend, mgot, True))
        send_group(2, rsend, rgot, g)

    each_group(group0, -1)

    def collect(phase, src, dst):
        each_group(lambda g: wait_group(phase, src, dst, g), -1)
        returned = jnp.concatenate([eight(dst, g) for g in range(groups)], axis=0)
        ids = jnp.concatenate([pgot_ids(g) for g in range(groups)], axis=0)
        ids_row = jnp.sum(jnp.where(eye, ids[:, 0:1], 0.0), axis=0, keepdims=True)
        block = fiota((BLOCKS, slots), 0)
        to_own = jnp.where(block == ownr[...], 1.0, 0.0).astype(BF16)
        to_target = jnp.where(block == ids_row, 1.0, 0.0).astype(BF16)
        rh, rm = parts2(returned)
        sh, sm = parts2(second[...])
        forces[...] = (plain(to_own, rh) + plain(to_own, rm)) + (
            plain(to_target, sh) + plain(to_target, sm)
        )

    def spread(out, base):
        for part in range(2):
            for k in range(BLOCKS):
                at = slice(k * WIDTH, (k + 1) * WIDTH)
                mask = iota((256, WIDTH), 0) == map_ref[0, 0, k : k + 1, :] // DEPTH
                for c in range(3):
                    force = forces[k : k + 1, c * WIDTH : (c + 1) * WIDTH]
                    high = force.astype(BF16).astype(F32)
                    kept = high if part == 0 else force - high
                    lhs[c, part, :, at] = jnp.where(mask, kept, 0.0).astype(BF16)
        cells = jnp.concatenate([ez[k] for k in range(BLOCKS)], axis=1)
        for c in range(3):
            total = lanes_t(lhs[c, 0], cells) + lanes_t(lhs[c, 1], cells)
            out[c, base : base + ROWS] = out[c, base : base + ROWS] + total.reshape(
                ROWS, COLS, DEPTH
            )

    near = min(16, nb)
    place_near, base_near = lax.rem(b, near), (b // near) * near
    far_count = (nb // near) * na
    place_far = (b // near) * na + a

    def peer_of(stage, other):
        if stage == 0:
            return (base_near + other, a)
        return ((other // na) * near + place_near, lax.rem(other, na))

    def ar_copy(n, stage, peer, slot):
        return pltpu.make_async_remote_copy(
            src_ref=arsend.at[n, stage], dst_ref=argot.at[n, stage, slot],
            send_sem=ar_send.at[n, stage, peer], recv_sem=ar_recv.at[n, stage, slot],
            device_id=peer_of(stage, peer), device_id_type=MESH,
        )

    def ar_start(n, stage, value):
        own, size = ((place_near, near), (place_far, far_count))[stage]
        arsend[n, stage] = value

        def step(t, carry):
            ar_copy(n, stage, wrap(own + t, size), own).start()
            return carry

        lax.fori_loop(1, size, step, 0)
        argot[n, stage, own] = value

    def ar_finish(n, stage):
        own, size = ((place_near, near), (place_far, far_count))[stage]

        def step(t, carry):
            other = wrap(own + t, size)
            copy = ar_copy(n, stage, other, other)
            copy.wait_recv()
            copy.wait_send()
            return carry

        lax.fori_loop(1, size, step, 0)
        total = argot[n, stage, 0]
        for k in range(1, size):
            total = total + argot[n, stage, k]
        return total

    def rows_of(*sums):
        row = iota((8, WIDTH), 0)
        value = jnp.zeros((8, WIDTH), F32)
        for k, s in enumerate(sums):
            folded = jnp.sum(s, axis=0, keepdims=True)
            folded = sum(
                folded[:, j : j + WIDTH] for j in range(0, folded.shape[1], WIDTH)
            )
            value = jnp.where(row == k, folded, value)
        return value

    def scalar(total, k):
        return jnp.sum(total[k : k + 1], axis=1, keepdims=True)

    def whole(vector, base):
        return [vector[c, base + i] for c in range(3) for i in range(ROWS)]

    collect(2, rsend, rgot)
    moves1[...] = moves1[...] + forces[...]
    moves_out(3, moves1, fsend, fgot)
    spread(qx, 1)
    for c in range(3):
        ysend1[0, c] = qx[c, 1 : ROWS + 1, COLS - 1, :]
        ysend1[1, c] = qx[c, 1 : ROWS + 1, 0, :]
    halos1 = [
        halo(6, qx.at[:, last], qx.at[:, 0], (up, a)),
        halo(7, qx.at[:, 1], qx.at[:, last + 1], (down, a)),
        halo(8, ysend1.at[0], ygot1.at[0], (b, right)),
        halo(9, ysend1.at[1], ygot1.at[1], (b, left)),
    ]
    for copy in halos1:
        copy.start()
    c_c = jnp.zeros((COLS, DEPTH), F32)
    for v in whole(cx, 1):
        c_c = c_c + v * v
    ar_start(0, 0, rows_of(c_c, c_ec, moves0[...] * forces[...]))
    for copy in halos1:
        copy.wait_recv()
    clear_edges((qx,), ygot1)
    elastic(qx, ygot1, q2, 0, ())
    ar_start(0, 1, ar_finish(0, 0))

    def group1(g):
        wait_group(3, fsend, fgot, g)
        store_eight(bsend, g, sides(g, fsend, fgot, False))
        send_group(4, bsend, bgot, g)

    each_group(group1, -1)

    total0 = ar_finish(0, 1)
    norm0 = scalar(total0, 0)
    step0 = norm0 / (scalar(total0, 1) + scalar(total0, 2))

    def products(i, sums):
        r_r, r_ar = sums
        for c in range(3):
            q = qx[c, i + 1]
            r = cx[c, i + 1] - step0 * q
            r_r = r_r + r * r
            r_ar = r_ar + r * (q - step0 * q2[c, i])
        return r_r, r_ar

    zero = jnp.zeros((COLS, DEPTH), F32)
    r_r, r_ar = lax.fori_loop(0, ROWS, products, (zero, zero))
    collect(4, bsend, bgot)
    r_moves = moves0[...] - step0 * moves1[...]
    ar_start(1, 0, rows_of(r_r, r_ar, -step0 * (r_moves * forces[...])))
    spread(q2, 0)
    ar_start(1, 1, ar_finish(1, 0))
    total1 = ar_finish(1, 1)
    norm1 = scalar(total1, 0)
    product = scalar(total1, 1) + scalar(total1, 2)
    ratio = norm1 / norm0
    step1 = norm1 / (product - ratio * norm1 / step0)
    on_first = step0 + step1 * (1.0 + ratio)
    on_second = step1 * step0

    def finish(i, carry):
        for c in range(3):
            v, q = cx[c, i + 1], qx[c, i + 1]
            outs[0, c, i] = on_first * v - on_second * q
            outs[1, c, i] = v - on_first * q + on_second * q2[c, i]
        return carry

    lax.fori_loop(0, ROWS, finish, 0)
    stores = [
        pltpu.make_async_copy(outs.at[0], disp_hbm, sem_out.at[0]),
        pltpu.make_async_copy(outs.at[1], res_hbm, sem_out.at[1]),
    ]
    for store in stores:
        store.start()
    for copy in halos0 + halos1:
        copy.wait_send()

    def drain(t, carry):
        peer = wrap(b + t, nb)
        for phase, (src, dst) in enumerate(
            ((psend, pgot), (msend, mgot), (rsend, rgot), (fsend, fgot), (bsend, bgot))
        ):
            a2a(phase, src, dst, peer).wait_send()
        return carry

    lax.fori_loop(1, nb, drain, 0)
    for store in stores:
        store.wait()


def on_device(nb, na, cotangent, shear, lame, inertia, points, counts, maps, pairs):
    slots = nb * CAP
    grid = (3, ROWS, COLS, DEPTH)
    near = min(16, nb)
    peers = max(near, (nb // near) * na)

    def buffers(width):
        return [pltpu.VMEM((nb, CAP, width), F32)] * 2

    scratch = [
        pltpu.VMEM((3, ROWS + 2, COLS, DEPTH), F32),
        pltpu.VMEM((3, ROWS + 2, COLS, DEPTH), F32),
        pltpu.VMEM(grid, F32),
        pltpu.VMEM((2, ROWS + 2, COLS, DEPTH), F32),
        pltpu.VMEM((ROWS, COLS, DEPTH), F32),
        pltpu.VMEM((6, 2, ROWS, COLS, DEPTH), F32),
        pltpu.VMEM((BLOCKS, DEPTH, WIDTH), BF16),
        pltpu.VMEM((768, DEPTH), BF16),
        pltpu.VMEM((768, DEPTH), BF16),
        pltpu.VMEM((3, 2, 256, BLOCKS * WIDTH), BF16),
        pltpu.VMEM((slots, 2 * WIDTH, WIDTH), BF16),
        pltpu.VMEM((BLOCKS, MOVE), F32),
        pltpu.VMEM((BLOCKS, MOVE), F32),
        pltpu.VMEM((WIDTH, MOVE), BF16),
        pltpu.VMEM((WIDTH, MOVE), BF16),
        pltpu.VMEM((WIDTH, 12 * WIDTH), BF16),
        pltpu.VMEM((slots, WIDTH), F32),
        pltpu.VMEM((slots, WIDTH), F32),
        pltpu.VMEM((1, slots), F32),
        pltpu.VMEM((slots, MOVE), F32),
        pltpu.VMEM((slots, WIDTH), F32),
        pltpu.VMEM((slots, WIDTH), F32),
        pltpu.VMEM((BLOCKS, MOVE), F32),
        *buffers(MOVE + WIDTH),
        *buffers(MOVE),
        *buffers(MOVE),
        *buffers(MOVE),
        *buffers(MOVE),
        pltpu.VMEM((2, 5, ROWS, DEPTH), F32),
        pltpu.VMEM((2, 5, ROWS, DEPTH), F32),
        pltpu.VMEM((2, 3, ROWS, DEPTH), F32),
        pltpu.VMEM((2, 3, ROWS, DEPTH), F32),
        pltpu.VMEM((2, 2, 8, WIDTH), F32),
        pltpu.VMEM((2, 2, peers, 8, WIDTH), F32),
        pltpu.VMEM((2,) + grid, F32),
        pltpu.SemaphoreType.DMA((4,)),
        pltpu.SemaphoreType.DMA((2,)),
        pltpu.SemaphoreType.DMA((5, nb)),
        pltpu.SemaphoreType.DMA((5, nb)),
        pltpu.SemaphoreType.DMA((10,)),
        pltpu.SemaphoreType.DMA((10,)),
        pltpu.SemaphoreType.DMA((2, 2, peers)),
        pltpu.SemaphoreType.DMA((2, 2, peers)),
    ]
    return pl.pallas_call(
        functools.partial(kernel, nb, na),
        out_shape=[jax.ShapeDtypeStruct(grid, F32)] * 2,
        in_specs=[pl.BlockSpec(memory_space=pl.ANY)] * 4
        + [
            pl.BlockSpec(memory_space=pltpu.VMEM),
            pl.BlockSpec(memory_space=pltpu.SMEM),
            pl.BlockSpec(memory_space=pltpu.VMEM),
            pl.BlockSpec(memory_space=pltpu.VMEM),
        ],
        out_specs=[pl.BlockSpec(memory_space=pl.ANY)] * 2,
        scratch_shapes=scratch,
        compiler_params=pltpu.CompilerParams(
            has_side_effects=True, vmem_limit_bytes=58 * 2**20
        ),
        name="adjoint_cg",
    )(cotangent, shear, lame, inertia, points, counts, maps, pairs[0, 0])


def solution(mesh):
    nb, na = mesh.shape["body"], mesh.shape["across"]
    split = P("body", "across")
    vector = P(None, "body", "across", None)
    return jax.shard_map(
        functools.partial(on_device, nb, na),
        mesh=mesh,
        in_specs=(vector, split, split, split, split, split, split, split),
        out_specs=(vector, vector),
        check_vma=False,
    )
```

```python
import functools

import jax
import jax.numpy as jnp
from jax import lax
from jax.experimental import pallas as pl
from jax.experimental.pallas import tpu as pltpu
from jax.sharding import PartitionSpec as P

MESH = pl.DeviceIdType.MESH
CAP = 4
ROWS, COLS, DEPTH = 8, 32, 256
BLOCKS, WIDTH = 16, 128
MOVE = 3 * WIDTH
F32, BF16 = jnp.float32, jnp.bfloat16
FAR = 100.0


def iota(shape, dim):
    return lax.broadcasted_iota(jnp.int32, shape, dim)


def fiota(shape, dim):
    return iota(shape, dim).astype(F32)


def parts2(x):
    high = x.astype(BF16)
    return high, (x - high.astype(F32)).astype(BF16)


def parts3(x):
    high = x.astype(BF16).astype(F32)
    rest = x - high
    mid = rest.astype(BF16).astype(F32)
    return high, mid, rest - mid


def lanes_t(a, b):
    return lax.dot_general(a, b, (((1,), (1,)), ((), ())), preferred_element_type=F32)


def plain(a, b):
    return jnp.dot(a, b, preferred_element_type=F32)


def kernel(
    nb, na,
    c_hbm, mu_hbm, lam_hbm, inertia_hbm, pts_ref, cnt_ref, map_ref, pair_ref,
    disp_hbm, res_hbm,
    cx, qx, q2, mx, inertia, fw, ez, vhm, lhs, ws,
    moves0, moves1, mparts, pparts, own3, tgtc, ownr, second, rowt, colt, forces,
    psend, pgot, msend, mgot, rsend, rgot, fsend, fgot, bsend, bgot,
    ysend, ygot, ysend1, ygot1, arsend, argot, outs,
    sem_in, sem_out, a2a_send, a2a_recv, halo_send, halo_recv, ar_send, ar_recv,
):
    b = lax.axis_index("body")
    a = lax.axis_index("across")
    slots = nb * CAP
    groups = nb // 2
    chunks = nb // 4
    me_q = b // 4

    def wrap(i, n):
        return lax.rem(i + n, n)

    loads = [
        pltpu.make_async_copy(c_hbm, cx.at[:, pl.ds(1, ROWS)], sem_in.at[0]),
        pltpu.make_async_copy(mu_hbm, mx.at[0, pl.ds(1, ROWS)], sem_in.at[1]),
        pltpu.make_async_copy(lam_hbm, mx.at[1, pl.ds(1, ROWS)], sem_in.at[2]),
        pltpu.make_async_copy(inertia_hbm, inertia, sem_in.at[3]),
    ]
    for load in loads:
        load.start()

    own_row, partner_row, target_row = (pair_ref[k].astype(F32) for k in range(3))
    sub, lane = iota((slots, slots), 0), iota((slots, slots), 1)
    eye = sub == lane
    partner_col = jnp.sum(jnp.where(eye, partner_row, 0.0), axis=1, keepdims=True)
    rank = jnp.sum(
        jnp.where((partner_col == partner_row) & (sub < lane), 1.0, 0.0), axis=0, keepdims=True
    )
    slot_row = partner_row * CAP + rank
    chosen = slot_row == sub.astype(F32)
    own_col = jnp.sum(jnp.where(chosen, own_row, 0.0), axis=1, keepdims=True)
    target_col = jnp.sum(jnp.where(chosen, target_row, 0.0), axis=1, keepdims=True)
    tgtc[...] = jnp.broadcast_to(target_col, (slots, WIDTH))
    ownr[...] = jnp.sum(jnp.where(eye, own_col, 0.0), axis=0, keepdims=True)

    block_id = iota((BLOCKS, WIDTH), 0)
    count = jnp.zeros((BLOCKS, WIDTH), jnp.int32)
    for k in range(BLOCKS):
        count = jnp.where(block_id == k, cnt_ref[0, 0, k], count)
    active = iota((BLOCKS, WIDTH), 1) < count
    far = jnp.where(lax.rem(block_id, 2) == 0, FAR, -FAR)
    coords = [
        jnp.where(active, pts_ref[0] - 0.5, far),
        pts_ref[1] - 0.5,
        pts_ref[2],
    ]
    pad16 = jnp.zeros((BLOCKS, WIDTH), F32)

    def store_parts(ref, tiles):
        for c, tile in enumerate(tiles):
            stacked = jnp.concatenate([*parts3(tile)] + [pad16] * 5, axis=0)
            ref[:, c * WIDTH : (c + 1) * WIDTH] = stacked.astype(BF16)

    store_parts(pparts, coords)
    lane8 = iota((8, WIDTH), 1)
    lane3 = jnp.where(lane8 < 3 * BLOCKS, lax.rem(lane8, BLOCKS), -1).astype(F32)
    sub8 = iota((8, WIDTH), 0)

    lanes = iota((slots, WIDTH), 1)
    lanes3 = jnp.where(lanes < 3 * BLOCKS, lax.rem(lanes, BLOCKS), -1).astype(F32)
    own3[...] = jnp.where(own_col == lanes3, 1.0, 0.0).astype(BF16)

    def select3(ids, ref):
        return plain(jnp.where(ids == lane3, 1.0, 0.0).astype(BF16), ref[...])

    def eight(ref, g):
        return jnp.concatenate([ref[2 * g], ref[2 * g + 1]], axis=0)

    def store_eight(ref, g, value):
        ref[2 * g] = value[:4]
        ref[2 * g + 1] = value[4:]

    def rows8(g):
        return pl.ds(pl.multiple_of(g * 8, 8), 8)

    def a2a(phase, src, dst, peer):
        return pltpu.make_async_remote_copy(
            src_ref=src.at[peer], dst_ref=dst.at[b],
            send_sem=a2a_send.at[phase], recv_sem=a2a_recv.at[phase, arrives(phase, me_q)],
            device_id=(peer, a), device_id_type=MESH,
        )

    def arrives(phase, q):
        return 0 if phase in (2, 4) else q

    def batch(phase, src, dst, q, first, count):
        at = pl.ds(first, count)
        return pltpu.make_async_remote_copy(
            src_ref=src.at[at], dst_ref=dst.at[at],
            send_sem=a2a_send.at[phase], recv_sem=a2a_recv.at[phase, arrives(phase, q)],
            device_id=(wrap(b + 1, nb), a), device_id_type=MESH,
        )

    def send_chunk(phase, src, dst, q):
        for h in range(4):
            peer = 4 * q + h

            @pl.when(peer != b)
            def _():
                a2a(phase, src, dst, peer).start()

            @pl.when(peer == b)
            def _():
                dst[peer] = src[peer]

    def wait_chunk(phase, src, dst, q):
        @pl.when(q != me_q)
        def _():
            batch(phase, src, dst, q, 4 * q, 4).wait_recv()

        @pl.when(q == me_q)
        def _():
            batch(phase, src, dst, q, 4 * q, 3).wait_recv()

    def each_chunk(body, sign):
        def step(t, carry):
            body(wrap(me_q + sign * t, chunks))
            return carry

        lax.fori_loop(0, chunks, step, 0)

    def store_all(ref, value):
        for k in range(nb):
            ref[k] = value[k * CAP : (k + 1) * CAP]

    store_all(psend, jnp.concatenate([plain(own3[...], pparts[...]), tgtc[...]], axis=1))
    each_chunk(lambda q: send_chunk(0, psend, pgot, q), 1)
    for load in loads:
        load.wait()
    up, down = wrap(b + 1, nb), wrap(b - 1, nb)
    right, left = wrap(a + 1, na), wrap(a - 1, na)

    def halo(k, src, dst, peer):
        return pltpu.make_async_remote_copy(
            src_ref=src, dst_ref=dst, send_sem=halo_send.at[k], recv_sem=halo_recv.at[k],
            device_id=peer, device_id_type=MESH,
        )

    last = ROWS
    for c in range(3):
        ysend[0, c] = cx[c, 1 : ROWS + 1, COLS - 1, :]
        ysend[1, c] = cx[c, 1 : ROWS + 1, 0, :]
    for m in range(2):
        ysend[0, 3 + m] = mx[m, 1 : ROWS + 1, COLS - 1, :]
        ysend[1, 3 + m] = mx[m, 1 : ROWS + 1, 0, :]
    halos0 = [
        halo(0, cx.at[:, last], cx.at[:, 0], (up, a)),
        halo(1, cx.at[:, 1], cx.at[:, last + 1], (down, a)),
        halo(2, mx.at[:, last], mx.at[:, 0], (up, a)),
        halo(3, mx.at[:, 1], mx.at[:, last + 1], (down, a)),
        halo(4, ysend.at[0], ygot.at[0], (b, right)),
        halo(5, ysend.at[1], ygot.at[1], (b, left)),
    ]
    for copy in halos0:
        copy.start()

    def map_row(k):
        pair = map_ref[0, 0, pl.ds(2 * k, 1), :], map_ref[0, 0, pl.ds(2 * k + 1, 1), :]
        return jnp.concatenate(pair, axis=1)

    def place(k, carry):
        z = lax.rem(map_row(k), DEPTH)
        ez[k] = jnp.where(iota((DEPTH, 2 * WIDTH), 0) == z, 1.0, 0.0).astype(BF16)
        return carry

    lax.fori_loop(0, BLOCKS // 2, place, 0)

    def pick(vector, base, moves):
        for c in range(3):
            flat = vector[c, base : base + ROWS].reshape(ROWS * COLS, DEPTH)
            at = slice(c * 256, (c + 1) * 256)
            vhm[at, :DEPTH], vhm[at, DEPTH:] = parts2(flat)

        def step(k, rows):
            picked = plain(vhm[...], jnp.concatenate([ez[k], ez[k]], axis=0))
            mask = iota((256, 2 * WIDTH), 0) == map_row(k) // DEPTH
            made = []
            for c in range(3):
                kept = jnp.where(mask, picked[c * 256 : (c + 1) * 256], 0.0)
                row = jnp.sum(kept, axis=0, keepdims=True)
                lower = jnp.where(block_id == 2 * k, row[:, :WIDTH], rows[c])
                made.append(jnp.where(block_id == 2 * k + 1, row[:, WIDTH:], lower))
            return tuple(made)

        rows = lax.fori_loop(0, BLOCKS // 2, step, (pad16,) * 3)
        moves[...] = jnp.concatenate(rows, axis=1)

    pick(cx, 1, moves0)

    def tiles(value):
        return [value[:, c * WIDTH : (c + 1) * WIDTH] for c in range(3)]

    def moves_out(phase, moves, src, dst):
        store_parts(mparts, tiles(moves[...]))

        store_all(src, plain(own3[...], mparts[...]))
        each_chunk(lambda q: send_chunk(phase, src, dst, q), 1)

    moves_out(1, moves0, msend, mgot)

    row32, lane256 = iota((COLS, DEPTH), 0), iota((COLS, DEPTH), 1)

    def clear_edges(xs, yhalo):
        @pl.when(b == 0)
        def _():
            for x in xs:
                x[:, 0] = jnp.zeros_like(x[:, 0])

        @pl.when(b == nb - 1)
        def _():
            for x in xs:
                x[:, last + 1] = jnp.zeros_like(x[:, last + 1])

        @pl.when(a == 0)
        def _():
            yhalo[0] = jnp.zeros_like(yhalo[0])

        @pl.when(a == na - 1)
        def _():
            yhalo[1] = jnp.zeros_like(yhalo[1])

    def beside(v, low, high):
        return (
            jnp.where(row32 == COLS - 1, high, pltpu.roll(v, COLS - 1, 0)),
            jnp.where(row32 == 0, low, pltpu.roll(v, 1, 0)),
            jnp.where(lane256 == DEPTH - 1, 0.0, pltpu.roll(v, DEPTH - 1, 1)),
            jnp.where(lane256 == 0, 0.0, pltpu.roll(v, 1, 1)),
        )

    def faces(i, carry):
        mu, lam = mx[0, i + 1], mx[1, i + 1]
        near_mu = (mx[0, i + 2], mx[0, i]) + beside(
            mu, ygot[0, 3, pl.ds(i, 1), :], ygot[1, 3, pl.ds(i, 1), :]
        )
        near_lam = (mx[1, i + 2], mx[1, i]) + beside(
            lam, ygot[0, 4, pl.ds(i, 1), :], ygot[1, 4, pl.ds(i, 1), :]
        )
        cut = nb // 4
        open_high = jnp.where((b == cut - 1) & (i == ROWS - 1), 0.0, 0.5)
        open_low = jnp.where((b == cut) & (i == 0), 0.0, 0.5)
        for k in range(6):
            half = (open_high, open_low, 0.5, 0.5, 0.5, 0.5)[k]
            plain_weight = half * (mu + near_mu[k])
            fw[k, 0, i] = plain_weight
            fw[k, 1, i] = 2.0 * plain_weight + half * (lam + near_lam[k])
        return carry

    def elastic(vector, yhalo, out, base, others):
        def plane(i, sums):
            sums = list(sums)
            for c in range(3):
                v = vector[c, i + 1]
                near = (vector[c, i + 2], vector[c, i]) + beside(
                    v, yhalo[0, c, pl.ds(i, 1), :], yhalo[1, c, pl.ds(i, 1), :]
                )
                value = inertia[i] * v
                for k in range(6):
                    value = value + fw[k, int(k // 2 == c), i] * (v - near[k])
                out[c, base + i] = value
                for n, other in enumerate(others):
                    sums[n] = sums[n] + value * other[c, i + 1]
            return tuple(sums)

        zero = jnp.zeros((COLS, DEPTH), F32)
        return lax.fori_loop(0, ROWS, plane, (zero,) * len(others))

    for copy in halos0:
        copy.wait_recv()
    clear_edges((cx, mx), ygot)
    lax.fori_loop(0, ROWS, faces, 0)
    (c_ec,) = elastic(cx, ygot, qx, 1, (cx,))
    pick(qx, 1, moves1)

    ones8 = jnp.ones((8, WIDTH), F32)

    def weigh(g):
        got = eight(pgot, g)
        ids = got[:, MOVE:]
        ys = tiles(select3(ids, pparts))
        pad = jnp.zeros((WIDTH - 24, WIDTH), F32)
        xs = jnp.concatenate(tiles(got) + [pad], axis=0).T
        for r in range(8):
            squared = None
            for c in range(3):
                apart = xs[:, 8 * c + r : 8 * c + r + 1] - ys[c][r : r + 1]
                squared = apart * apart if squared is None else squared + apart * apart
            squared = jnp.minimum(squared, 1.0)
            inverse = 1.0 / squared
            weight = 0.005 * (inverse * (inverse + 2.0) - 3.0) - 0.01 * jnp.log(squared)
            high, low = parts2(weight)
            ws[g * 8 + r, 0:WIDTH] = high
            ws[g * 8 + r, WIDTH : 2 * WIDTH] = low

    def halves(value, extra):
        rows = []
        for tile in tiles(value):
            high = tile.astype(BF16).astype(F32)
            rows += [high, tile - high]
        return rows + extra

    def only(rows, keep):
        kept = [jnp.where(keep, row, 0.0) for row in rows]
        return jnp.concatenate(kept, axis=0).astype(BF16)

    def sides(g, dst, mine, first_phase):
        got = eight(dst, g)
        extra = [ones8, ones8] if first_phase else []
        v_rows, u_rows = halves(got, extra), halves(mine, extra)
        w = [ws[g * 8 + r] for r in range(8)]
        v_side, w_side = [], []
        for q in range(4):
            kept = only(v_rows, lax.rem(sub8, 4) == q)
            v_side += [kept, kept]
            w_side.append(jnp.concatenate([w[q], w[q + 4]], axis=1))
        to_second = plain(jnp.concatenate(v_side, axis=1), jnp.concatenate(w_side, axis=0))
        u_side = jnp.concatenate([only(u_rows, sub8 == r) for r in range(8)], axis=1)
        to_first = lanes_t(u_side, jnp.concatenate(w, axis=1))
        to_first = to_first[:, :WIDTH] + to_first[:, WIDTH:]
        into_second, into_first = [], []
        for k in range(len(v_rows)):
            at = slice(8 * k, 8 * k + 8)
            into_second.append(
                jnp.where(sub8 < 4, to_second[at, :WIDTH], to_second[at, WIDTH:])
            )
            into_first.append(to_first[at])
        at = rows8(g)
        if first_phase:
            rowt[at], colt[at] = into_first[6], into_second[6]
        row_total, col_total = rowt[at], colt[at]

        def force(move, total, parts, c):
            return move * total - (parts[2 * c] + parts[2 * c + 1])

        second[at] = jnp.concatenate(
            [force(u, col_total, into_second, c) for c, u in enumerate(tiles(mine))], axis=1
        )
        return jnp.concatenate(
            [force(v, row_total, into_first, c) for c, v in enumerate(tiles(got))], axis=1
        )

    def pgot_ids(g):
        return jnp.concatenate([pgot[2 * g, :, MOVE:], pgot[2 * g + 1, :, MOVE:]], axis=0)

    def chunk0(q):
        wait_chunk(0, psend, pgot, q)
        for g in (2 * q, 2 * q + 1):
            weigh(g)
        wait_chunk(1, msend, mgot, q)
        for g in (2 * q, 2 * q + 1):
            mine = select3(pgot_ids(g), mparts)
            store_eight(rsend, g, sides(g, mgot, mine, True))
        send_chunk(2, rsend, rgot, q)

    each_chunk(chunk0, -1)

    def collect(phase, src, dst):
        batch(phase, src, dst, 0, 0, nb - 1).wait_recv()
        returned = jnp.concatenate([eight(dst, g) for g in range(groups)], axis=0)
        ids = jnp.concatenate([pgot_ids(g) for g in range(groups)], axis=0)
        ids_row = jnp.sum(jnp.where(eye, ids[:, 0:1], 0.0), axis=0, keepdims=True)
        block = fiota((BLOCKS, slots), 0)
        to_own = jnp.where(block == ownr[...], 1.0, 0.0).astype(BF16)
        to_target = jnp.where(block == ids_row, 1.0, 0.0).astype(BF16)
        rh, rm = parts2(returned)
        sh, sm = parts2(second[...])
        forces[...] = (plain(to_own, rh) + plain(to_own, rm)) + (
            plain(to_target, sh) + plain(to_target, sm)
        )

    def spread(out, base):
        for part in range(2):
            for k in range(BLOCKS):
                at = slice(k * WIDTH, (k + 1) * WIDTH)
                mask = iota((256, WIDTH), 0) == map_ref[0, 0, k : k + 1, :] // DEPTH
                for c in range(3):
                    force = forces[k : k + 1, c * WIDTH : (c + 1) * WIDTH]
                    high = force.astype(BF16).astype(F32)
                    kept = high if part == 0 else force - high
                    lhs[c, part, :, at] = jnp.where(mask, kept, 0.0).astype(BF16)
        cells = jnp.concatenate([ez[k] for k in range(BLOCKS // 2)], axis=1)
        for c in range(3):
            total = lanes_t(lhs[c, 0], cells) + lanes_t(lhs[c, 1], cells)
            out[c, base : base + ROWS] = out[c, base : base + ROWS] + total.reshape(
                ROWS, COLS, DEPTH
            )

    near = min(16, nb)
    place_near, base_near = lax.rem(b, near), (b // near) * near
    far_count = (nb // near) * na
    place_far = (b // near) * na + a

    def peer_of(stage, other):
        if stage == 0:
            return (base_near + other, a)
        return ((other // na) * near + place_near, lax.rem(other, na))

    def ar_copy(n, stage, peer, slot):
        return pltpu.make_async_remote_copy(
            src_ref=arsend.at[n, stage], dst_ref=argot.at[n, stage, slot],
            send_sem=ar_send.at[n, stage], recv_sem=ar_recv.at[n, stage],
            device_id=peer_of(stage, peer), device_id_type=MESH,
        )

    def ar_start(n, stage, value):
        own, size = ((place_near, near), (place_far, far_count))[stage]
        arsend[n, stage] = value

        def step(t, carry):
            ar_copy(n, stage, wrap(own + t, size), own).start()
            return carry

        lax.fori_loop(1, size, step, 0)
        argot[n, stage, own] = value

    def ar_finish(n, stage):
        own, size = ((place_near, near), (place_far, far_count))[stage]

        for k in range(2):
            at = pl.ds(0, size - 1)
            arrived = pltpu.make_async_remote_copy(
                src_ref=argot.at[n, stage, at], dst_ref=argot.at[n, stage, at],
                send_sem=ar_send.at[n, stage], recv_sem=ar_recv.at[n, stage],
                device_id=peer_of(stage, wrap(own + 1, size)), device_id_type=MESH,
            )
            (arrived.wait_recv, arrived.wait_send)[k]()
        total = argot[n, stage, 0]
        for k in range(1, size):
            total = total + argot[n, stage, k]
        return total

    def rows_of(*sums):
        row = iota((8, WIDTH), 0)
        value = jnp.zeros((8, WIDTH), F32)
        for k, s in enumerate(sums):
            folded = jnp.sum(s, axis=0, keepdims=True)
            folded = sum(
                folded[:, j : j + WIDTH] for j in range(0, folded.shape[1], WIDTH)
            )
            value = jnp.where(row == k, folded, value)
        return value

    def scalar(total, k):
        return jnp.sum(total[k : k + 1], axis=1, keepdims=True)

    def whole(vector, base):
        return [vector[c, base + i] for c in range(3) for i in range(ROWS)]

    collect(2, rsend, rgot)
    moves1[...] = moves1[...] + forces[...]
    moves_out(3, moves1, fsend, fgot)
    spread(qx, 1)
    for c in range(3):
        ysend1[0, c] = qx[c, 1 : ROWS + 1, COLS - 1, :]
        ysend1[1, c] = qx[c, 1 : ROWS + 1, 0, :]
    halos1 = [
        halo(6, qx.at[:, last], qx.at[:, 0], (up, a)),
        halo(7, qx.at[:, 1], qx.at[:, last + 1], (down, a)),
        halo(8, ysend1.at[0], ygot1.at[0], (b, right)),
        halo(9, ysend1.at[1], ygot1.at[1], (b, left)),
    ]
    for copy in halos1:
        copy.start()
    c_c = jnp.zeros((COLS, DEPTH), F32)
    for v in whole(cx, 1):
        c_c = c_c + v * v
    ar_start(0, 0, rows_of(c_c, c_ec, moves0[...] * forces[...]))
    for copy in halos1:
        copy.wait_recv()
    clear_edges((qx,), ygot1)
    elastic(qx, ygot1, q2, 0, ())
    ar_start(0, 1, ar_finish(0, 0))

    def chunk1(q):
        wait_chunk(3, fsend, fgot, q)
        for g in (2 * q, 2 * q + 1):
            mine = select3(pgot_ids(g), mparts)
            store_eight(bsend, g, sides(g, fgot, mine, False))
        send_chunk(4, bsend, bgot, q)

    each_chunk(chunk1, -1)

    total0 = ar_finish(0, 1)
    norm0 = scalar(total0, 0)
    step0 = norm0 / (scalar(total0, 1) + scalar(total0, 2))

    def products(i, sums):
        r_r, r_ar = sums
        for c in range(3):
            q = qx[c, i + 1]
            r = cx[c, i + 1] - step0 * q
            r_r = r_r + r * r
            r_ar = r_ar + r * (q - step0 * q2[c, i])
        return r_r, r_ar

    zero = jnp.zeros((COLS, DEPTH), F32)
    r_r, r_ar = lax.fori_loop(0, ROWS, products, (zero, zero))
    collect(4, bsend, bgot)
    r_moves = moves0[...] - step0 * moves1[...]
    ar_start(1, 0, rows_of(r_r, r_ar, -step0 * (r_moves * forces[...])))
    spread(q2, 0)
    ar_start(1, 1, ar_finish(1, 0))
    total1 = ar_finish(1, 1)
    norm1 = scalar(total1, 0)
    product = scalar(total1, 1) + scalar(total1, 2)
    ratio = norm1 / norm0
    step1 = norm1 / (product - ratio * norm1 / step0)
    on_first = step0 + step1 * (1.0 + ratio)
    on_second = step1 * step0

    def finish(i, carry):
        for c in range(3):
            v, q = cx[c, i + 1], qx[c, i + 1]
            outs[0, c, i] = on_first * v - on_second * q
            outs[1, c, i] = v - on_first * q + on_second * q2[c, i]
        return carry

    lax.fori_loop(0, ROWS, finish, 0)
    stores = [
        pltpu.make_async_copy(outs.at[0], disp_hbm, sem_out.at[0]),
        pltpu.make_async_copy(outs.at[1], res_hbm, sem_out.at[1]),
    ]
    for store in stores:
        store.start()
    for copy in halos0 + halos1:
        copy.wait_send()

    for phase, (src, dst) in enumerate(
        ((psend, pgot), (msend, mgot), (rsend, rgot), (fsend, fgot), (bsend, bgot))
    ):
        batch(phase, src, dst, 0, 0, nb - 1).wait_send()
    for store in stores:
        store.wait()


def on_device(nb, na, cotangent, shear, lame, inertia, points, counts, maps, pairs):
    slots = nb * CAP
    grid = (3, ROWS, COLS, DEPTH)
    near = min(16, nb)
    peers = max(near, (nb // near) * na)

    def buffers(width):
        return [pltpu.VMEM((nb, CAP, width), F32)] * 2

    scratch = [
        pltpu.VMEM((3, ROWS + 2, COLS, DEPTH), F32),
        pltpu.VMEM((3, ROWS + 2, COLS, DEPTH), F32),
        pltpu.VMEM(grid, F32),
        pltpu.VMEM((2, ROWS + 2, COLS, DEPTH), F32),
        pltpu.VMEM((ROWS, COLS, DEPTH), F32),
        pltpu.VMEM((6, 2, ROWS, COLS, DEPTH), F32),
        pltpu.VMEM((BLOCKS // 2, DEPTH, 2 * WIDTH), BF16),
        pltpu.VMEM((768, 2 * DEPTH), BF16),
        pltpu.VMEM((3, 2, 256, BLOCKS * WIDTH), BF16),
        pltpu.VMEM((slots, 2 * WIDTH, WIDTH), BF16),
        pltpu.VMEM((BLOCKS, MOVE), F32),
        pltpu.VMEM((BLOCKS, MOVE), F32),
        pltpu.VMEM((WIDTH, MOVE), BF16),
        pltpu.VMEM((WIDTH, MOVE), BF16),
        pltpu.VMEM((slots, WIDTH), BF16),
        pltpu.VMEM((slots, WIDTH), F32),
        pltpu.VMEM((1, slots), F32),
        pltpu.VMEM((slots, MOVE), F32),
        pltpu.VMEM((slots, WIDTH), F32),
        pltpu.VMEM((slots, WIDTH), F32),
        pltpu.VMEM((BLOCKS, MOVE), F32),
        *buffers(MOVE + WIDTH),
        *buffers(MOVE),
        *buffers(MOVE),
        *buffers(MOVE),
        *buffers(MOVE),
        pltpu.VMEM((2, 5, ROWS, DEPTH), F32),
        pltpu.VMEM((2, 5, ROWS, DEPTH), F32),
        pltpu.VMEM((2, 3, ROWS, DEPTH), F32),
        pltpu.VMEM((2, 3, ROWS, DEPTH), F32),
        pltpu.VMEM((2, 2, 8, WIDTH), F32),
        pltpu.VMEM((2, 2, peers, 8, WIDTH), F32),
        pltpu.VMEM((2,) + grid, F32),
        pltpu.SemaphoreType.DMA((4,)),
        pltpu.SemaphoreType.DMA((2,)),
        pltpu.SemaphoreType.DMA((5,)),
        pltpu.SemaphoreType.DMA((5, nb // 4)),
        pltpu.SemaphoreType.DMA((10,)),
        pltpu.SemaphoreType.DMA((10,)),
        pltpu.SemaphoreType.DMA((2, 2)),
        pltpu.SemaphoreType.DMA((2, 2)),
    ]
    return pl.pallas_call(
        functools.partial(kernel, nb, na),
        out_shape=[jax.ShapeDtypeStruct(grid, F32)] * 2,
        in_specs=[pl.BlockSpec(memory_space=pl.ANY)] * 4
        + [
            pl.BlockSpec(memory_space=pltpu.VMEM),
            pl.BlockSpec(memory_space=pltpu.SMEM),
            pl.BlockSpec(memory_space=pltpu.VMEM),
            pl.BlockSpec(memory_space=pltpu.VMEM),
        ],
        out_specs=[pl.BlockSpec(memory_space=pl.ANY)] * 2,
        scratch_shapes=scratch,
        compiler_params=pltpu.CompilerParams(
            has_side_effects=True, vmem_limit_bytes=58 * 2**20
        ),
        name="adjoint_cg",
    )(
        cotangent, shear, lame, inertia,
        points[0, 0].transpose(1, 0, 2), counts, maps, pairs[0].transpose(1, 0, 2),
    )


def solution(mesh):
    nb, na = mesh.shape["body"], mesh.shape["across"]
    split = P("body", "across")
    vector = P(None, "body", "across", None)
    return jax.shard_map(
        functools.partial(on_device, nb, na),
        mesh=mesh,
        in_specs=(vector, split, split, split, split, split, split, split),
        out_specs=(vector, vector),
        check_vma=False,
    )
```

```python
import functools

import jax
import jax.numpy as jnp
from jax import lax
from jax.experimental import pallas as pl
from jax.experimental.pallas import tpu as pltpu
from jax.sharding import PartitionSpec as P

MESH = pl.DeviceIdType.MESH
CAP = 4
ROWS, COLS, DEPTH = 8, 32, 256
BLOCKS, WIDTH = 16, 128
MOVE = 3 * WIDTH
F32, BF16 = jnp.float32, jnp.bfloat16
FAR = 100.0


def iota(shape, dim):
    return lax.broadcasted_iota(jnp.int32, shape, dim)


def fiota(shape, dim):
    return iota(shape, dim).astype(F32)


def parts2(x):
    high = x.astype(BF16)
    return high, (x - high.astype(F32)).astype(BF16)


def parts3(x):
    high = x.astype(BF16).astype(F32)
    rest = x - high
    mid = rest.astype(BF16).astype(F32)
    return high, mid, rest - mid


def lanes_t(a, b):
    return lax.dot_general(a, b, (((1,), (1,)), ((), ())), preferred_element_type=F32)


def plain(a, b):
    return jnp.dot(a, b, preferred_element_type=F32)


def kernel(
    nb, na,
    c_hbm, mu_hbm, lam_hbm, inertia_hbm, pts_ref, cnt_ref, map_ref, pair_ref,
    q1_hbm, q2_hbm, coef_ref,
    cx, qx, q2, mx, inertia, fw, ez, vhm, lhs, ws,
    moves0, moves1, mparts, pparts, own3, tgtc, ownr, second, rowt, colt, forces,
    psend, pgot, msend, mgot, rsend, rgot, fsend, fgot, bsend, bgot,
    ysend, ygot, ysend1, ygot1, arsend, argot,
    sem_in, sem_out, a2a_send, a2a_recv, halo_send, halo_recv, ar_send, ar_recv,
):
    b = lax.axis_index("body")
    a = lax.axis_index("across")
    slots = nb * CAP
    groups = nb // 2
    chunks = nb // 4
    me_q = b // 4

    def wrap(i, n):
        return lax.rem(i + n, n)

    near = min(16, nb)
    place_near, base_near = lax.rem(b, near), (b // near) * near
    barrier = pltpu.get_barrier_semaphore()

    def greet(peer):
        pl.semaphore_signal(barrier, inc=1, device_id=peer, device_id_type=MESH)

    def greet_body(t, carry):
        greet((wrap(b + t, nb), a))
        return carry

    lax.fori_loop(1, nb, greet_body, 0)
    for t in range(1, na):
        for k in range(nb // near):
            greet((k * near + place_near, wrap(a + t, na)))

    loads = [
        pltpu.make_async_copy(c_hbm, cx.at[:, pl.ds(1, ROWS)], sem_in.at[0]),
        pltpu.make_async_copy(mu_hbm, mx.at[0, pl.ds(1, ROWS)], sem_in.at[1]),
        pltpu.make_async_copy(lam_hbm, mx.at[1, pl.ds(1, ROWS)], sem_in.at[2]),
        pltpu.make_async_copy(inertia_hbm, inertia, sem_in.at[3]),
    ]
    for load in loads:
        load.start()

    own_row, partner_row, target_row = (pair_ref[k].astype(F32) for k in range(3))
    sub, lane = iota((slots, slots), 0), iota((slots, slots), 1)
    eye = sub == lane
    partner_col = jnp.sum(jnp.where(eye, partner_row, 0.0), axis=1, keepdims=True)
    rank = jnp.sum(
        jnp.where((partner_col == partner_row) & (sub < lane), 1.0, 0.0), axis=0, keepdims=True
    )
    slot_row = partner_row * CAP + rank
    chosen = slot_row == sub.astype(F32)
    own_col = jnp.sum(jnp.where(chosen, own_row, 0.0), axis=1, keepdims=True)
    target_col = jnp.sum(jnp.where(chosen, target_row, 0.0), axis=1, keepdims=True)
    tgtc[...] = jnp.broadcast_to(target_col, (slots, WIDTH))
    ownr[...] = jnp.sum(jnp.where(eye, own_col, 0.0), axis=0, keepdims=True)

    block_id = iota((BLOCKS, WIDTH), 0)
    count = jnp.zeros((BLOCKS, WIDTH), jnp.int32)
    for k in range(BLOCKS):
        count = jnp.where(block_id == k, cnt_ref[0, 0, k], count)
    active = iota((BLOCKS, WIDTH), 1) < count
    far = jnp.where(lax.rem(block_id, 2) == 0, FAR, -FAR)
    coords = [
        jnp.where(active, pts_ref[0] - 0.5, far),
        pts_ref[1] - 0.5,
        pts_ref[2],
    ]
    pad16 = jnp.zeros((BLOCKS, WIDTH), F32)

    def store_parts(ref, tiles):
        for c, tile in enumerate(tiles):
            stacked = jnp.concatenate([*parts3(tile)] + [pad16] * 5, axis=0)
            ref[:, c * WIDTH : (c + 1) * WIDTH] = stacked.astype(BF16)

    store_parts(pparts, coords)
    lane8 = iota((8, WIDTH), 1)
    lane3 = jnp.where(lane8 < 3 * BLOCKS, lax.rem(lane8, BLOCKS), -1).astype(F32)
    sub8 = iota((8, WIDTH), 0)

    lanes = iota((slots, WIDTH), 1)
    lanes3 = jnp.where(lanes < 3 * BLOCKS, lax.rem(lanes, BLOCKS), -1).astype(F32)
    own3[...] = jnp.where(own_col == lanes3, 1.0, 0.0).astype(BF16)

    def select3(ids, ref):
        return plain(jnp.where(ids == lane3, 1.0, 0.0).astype(BF16), ref[...])

    def eight(ref, g):
        return jnp.concatenate([ref[2 * g], ref[2 * g + 1]], axis=0)

    def store_eight(ref, g, value):
        ref[2 * g] = value[:4]
        ref[2 * g + 1] = value[4:]

    def rows8(g):
        return pl.ds(pl.multiple_of(g * 8, 8), 8)

    def a2a(phase, src, dst, peer):
        return pltpu.make_async_remote_copy(
            src_ref=src.at[peer], dst_ref=dst.at[b],
            send_sem=a2a_send.at[phase], recv_sem=a2a_recv.at[phase, arrives(phase, me_q)],
            device_id=(peer, a), device_id_type=MESH,
        )

    def arrives(phase, q):
        return 0 if phase in (2, 4) else q

    def batch(phase, src, dst, q, first, count):
        at = pl.ds(first, count)
        return pltpu.make_async_remote_copy(
            src_ref=src.at[at], dst_ref=dst.at[at],
            send_sem=a2a_send.at[phase], recv_sem=a2a_recv.at[phase, arrives(phase, q)],
            device_id=(wrap(b + 1, nb), a), device_id_type=MESH,
        )

    def send_chunk(phase, src, dst, q):
        for h in range(4):
            peer = 4 * q + h

            @pl.when(peer != b)
            def _():
                a2a(phase, src, dst, peer).start()

            @pl.when(peer == b)
            def _():
                dst[peer] = src[peer]

    def wait_chunk(phase, src, dst, q):
        @pl.when(q != me_q)
        def _():
            batch(phase, src, dst, q, 4 * q, 4).wait_recv()

        @pl.when(q == me_q)
        def _():
            batch(phase, src, dst, q, 4 * q, 3).wait_recv()

    def each_chunk(body, sign, start=0, stop=nb // 4):
        def step(t, carry):
            body(wrap(me_q + sign * t, chunks))
            return carry

        lax.fori_loop(start, stop, step, 0)

    def store_all(ref, value):
        for k in range(nb):
            ref[k] = value[k * CAP : (k + 1) * CAP]

    store_all(psend, jnp.concatenate([plain(own3[...], pparts[...]), tgtc[...]], axis=1))
    def map_row(k):
        pair = map_ref[0, 0, pl.ds(2 * k, 1), :], map_ref[0, 0, pl.ds(2 * k + 1, 1), :]
        return jnp.concatenate(pair, axis=1)

    def place(k, carry):
        z = lax.rem(map_row(k), DEPTH)
        ez[k] = jnp.where(iota((DEPTH, 2 * WIDTH), 0) == z, 1.0, 0.0).astype(BF16)
        return carry

    lax.fori_loop(0, BLOCKS // 2, place, 0)

    pl.semaphore_wait(barrier, nb - 1 + (na - 1) * (nb // near))
    each_chunk(lambda q: send_chunk(0, psend, pgot, q), 1)
    for load in loads:
        load.wait()
    up, down = wrap(b + 1, nb), wrap(b - 1, nb)
    right, left = wrap(a + 1, na), wrap(a - 1, na)

    def halo(k, src, dst, peer):
        return pltpu.make_async_remote_copy(
            src_ref=src, dst_ref=dst, send_sem=halo_send.at[k], recv_sem=halo_recv.at[k],
            device_id=peer, device_id_type=MESH,
        )

    last = ROWS
    for c in range(3):
        ysend[0, c] = cx[c, 1 : ROWS + 1, COLS - 1, :]
        ysend[1, c] = cx[c, 1 : ROWS + 1, 0, :]
    for m in range(2):
        ysend[0, 3 + m] = mx[m, 1 : ROWS + 1, COLS - 1, :]
        ysend[1, 3 + m] = mx[m, 1 : ROWS + 1, 0, :]
    halos0 = [
        halo(0, cx.at[:, last], cx.at[:, 0], (up, a)),
        halo(1, cx.at[:, 1], cx.at[:, last + 1], (down, a)),
        halo(2, mx.at[:, last], mx.at[:, 0], (up, a)),
        halo(3, mx.at[:, 1], mx.at[:, last + 1], (down, a)),
        halo(4, ysend.at[0], ygot.at[0], (b, right)),
        halo(5, ysend.at[1], ygot.at[1], (b, left)),
    ]
    for copy in halos0:
        copy.start()

    def pick(vector, base, moves):
        for c in range(3):
            flat = vector[c, base : base + ROWS].reshape(ROWS * COLS, DEPTH)
            at = slice(c * 256, (c + 1) * 256)
            vhm[at, :DEPTH], vhm[at, DEPTH:] = parts2(flat)

        def step(k, rows):
            picked = plain(vhm[...], jnp.concatenate([ez[k], ez[k]], axis=0))
            mask = iota((256, 2 * WIDTH), 0) == map_row(k) // DEPTH
            made = []
            for c in range(3):
                kept = jnp.where(mask, picked[c * 256 : (c + 1) * 256], 0.0)
                row = jnp.sum(kept, axis=0, keepdims=True)
                lower = jnp.where(block_id == 2 * k, row[:, :WIDTH], rows[c])
                made.append(jnp.where(block_id == 2 * k + 1, row[:, WIDTH:], lower))
            return tuple(made)

        rows = lax.fori_loop(0, BLOCKS // 2, step, (pad16,) * 3)
        moves[...] = jnp.concatenate(rows, axis=1)

    pick(cx, 1, moves0)

    def tiles(value):
        return [value[:, c * WIDTH : (c + 1) * WIDTH] for c in range(3)]

    def moves_out(phase, moves, src, dst):
        store_parts(mparts, tiles(moves[...]))

        store_all(src, plain(own3[...], mparts[...]))
        each_chunk(lambda q: send_chunk(phase, src, dst, q), 1)

    moves_out(1, moves0, msend, mgot)

    row32, lane256 = iota((COLS, DEPTH), 0), iota((COLS, DEPTH), 1)

    def clear_edges(xs, yhalo):
        @pl.when(b == 0)
        def _():
            for x in xs:
                x[:, 0] = jnp.zeros_like(x[:, 0])

        @pl.when(b == nb - 1)
        def _():
            for x in xs:
                x[:, last + 1] = jnp.zeros_like(x[:, last + 1])

        @pl.when(a == 0)
        def _():
            yhalo[0] = jnp.zeros_like(yhalo[0])

        @pl.when(a == na - 1)
        def _():
            yhalo[1] = jnp.zeros_like(yhalo[1])

    def beside(v, low, high):
        return (
            jnp.where(row32 == COLS - 1, high, pltpu.roll(v, COLS - 1, 0)),
            jnp.where(row32 == 0, low, pltpu.roll(v, 1, 0)),
            jnp.where(lane256 == DEPTH - 1, 0.0, pltpu.roll(v, DEPTH - 1, 1)),
            jnp.where(lane256 == 0, 0.0, pltpu.roll(v, 1, 1)),
        )

    def faces(i, carry):
        mu, lam = mx[0, i + 1], mx[1, i + 1]
        near_mu = (mx[0, i + 2], mx[0, i]) + beside(
            mu, ygot[0, 3, pl.ds(i, 1), :], ygot[1, 3, pl.ds(i, 1), :]
        )
        near_lam = (mx[1, i + 2], mx[1, i]) + beside(
            lam, ygot[0, 4, pl.ds(i, 1), :], ygot[1, 4, pl.ds(i, 1), :]
        )
        cut = nb // 4
        open_high = jnp.where((b == cut - 1) & (i == ROWS - 1), 0.0, 0.5)
        open_low = jnp.where((b == cut) & (i == 0), 0.0, 0.5)
        for k in range(6):
            half = (open_high, open_low, 0.5, 0.5, 0.5, 0.5)[k]
            plain_weight = half * (mu + near_mu[k])
            fw[k, 0, i] = plain_weight
            fw[k, 1, i] = 2.0 * plain_weight + half * (lam + near_lam[k])
        return carry

    def elastic(vector, yhalo, out, base, others):
        def plane(i, sums):
            sums = list(sums)
            for c in range(3):
                v = vector[c, i + 1]
                near = (vector[c, i + 2], vector[c, i]) + beside(
                    v, yhalo[0, c, pl.ds(i, 1), :], yhalo[1, c, pl.ds(i, 1), :]
                )
                value = inertia[i] * v
                for k in range(6):
                    value = value + fw[k, int(k // 2 == c), i] * (v - near[k])
                out[c, base + i] = value
                for n, other in enumerate(others):
                    sums[n] = sums[n] + value * other[c, i + 1]
            return tuple(sums)

        zero = jnp.zeros((COLS, DEPTH), F32)
        return lax.fori_loop(0, ROWS, plane, (zero,) * len(others))

    ones8 = jnp.ones((8, WIDTH), F32)

    def weigh(g):
        got = eight(pgot, g)
        ids = got[:, MOVE:]
        ys = tiles(select3(ids, pparts))
        pad = jnp.zeros((WIDTH - 24, WIDTH), F32)
        xs = jnp.concatenate(tiles(got) + [pad], axis=0).T
        for r in range(8):
            squared = None
            for c in range(3):
                apart = xs[:, 8 * c + r : 8 * c + r + 1] - ys[c][r : r + 1]
                squared = apart * apart if squared is None else squared + apart * apart
            squared = jnp.minimum(squared, 1.0)
            inverse = 1.0 / squared
            weight = 0.005 * (inverse * (inverse + 2.0) - 3.0) - 0.01 * jnp.log(squared)
            high, low = parts2(weight)
            ws[g * 8 + r, 0:WIDTH] = high
            ws[g * 8 + r, WIDTH : 2 * WIDTH] = low

    def halves(value, extra):
        rows = []
        for tile in tiles(value):
            high = tile.astype(BF16).astype(F32)
            rows += [high, tile - high]
        return rows + extra

    def only(rows, keep):
        kept = [jnp.where(keep, row, 0.0) for row in rows]
        return jnp.concatenate(kept, axis=0).astype(BF16)

    def sides(g, dst, mine, first_phase):
        got = eight(dst, g)
        extra = [ones8, ones8] if first_phase else []
        v_rows, u_rows = halves(got, extra), halves(mine, extra)
        w = [ws[g * 8 + r] for r in range(8)]
        v_side, w_side = [], []
        for q in range(4):
            kept = only(v_rows, lax.rem(sub8, 4) == q)
            v_side += [kept, kept]
            w_side.append(jnp.concatenate([w[q], w[q + 4]], axis=1))
        to_second = plain(jnp.concatenate(v_side, axis=1), jnp.concatenate(w_side, axis=0))
        u_side = jnp.concatenate([only(u_rows, sub8 == r) for r in range(8)], axis=1)
        to_first = lanes_t(u_side, jnp.concatenate(w, axis=1))
        to_first = to_first[:, :WIDTH] + to_first[:, WIDTH:]
        into_second, into_first = [], []
        for k in range(len(v_rows)):
            at = slice(8 * k, 8 * k + 8)
            into_second.append(
                jnp.where(sub8 < 4, to_second[at, :WIDTH], to_second[at, WIDTH:])
            )
            into_first.append(to_first[at])
        at = rows8(g)
        if first_phase:
            rowt[at], colt[at] = into_first[6], into_second[6]
        row_total, col_total = rowt[at], colt[at]

        def force(move, total, parts, c):
            return move * total - (parts[2 * c] + parts[2 * c + 1])

        second[at] = jnp.concatenate(
            [force(u, col_total, into_second, c) for c, u in enumerate(tiles(mine))], axis=1
        )
        return jnp.concatenate(
            [force(v, row_total, into_first, c) for c, v in enumerate(tiles(got))], axis=1
        )

    def pgot_ids(g):
        return jnp.concatenate([pgot[2 * g, :, MOVE:], pgot[2 * g + 1, :, MOVE:]], axis=0)

    def chunk0(q):
        wait_chunk(0, psend, pgot, q)
        for g in (2 * q, 2 * q + 1):
            weigh(g)
        wait_chunk(1, msend, mgot, q)
        for g in (2 * q, 2 * q + 1):
            mine = select3(pgot_ids(g), mparts)
            store_eight(rsend, g, sides(g, mgot, mine, True))
        send_chunk(2, rsend, rgot, q)

    each_chunk(chunk0, -1)

    for copy in halos0:
        copy.wait_recv()
    clear_edges((cx, mx), ygot)
    lax.fori_loop(0, ROWS, faces, 0)
    (c_ec,) = elastic(cx, ygot, qx, 1, (cx,))
    pick(qx, 1, moves1)
    c_c = jnp.zeros((COLS, DEPTH), F32)
    for c in range(3):
        for i in range(ROWS):
            c_c = c_c + cx[c, i + 1] * cx[c, i + 1]


    def collect(phase, src, dst):
        batch(phase, src, dst, 0, 0, nb - 1).wait_recv()
        returned = jnp.concatenate([eight(dst, g) for g in range(groups)], axis=0)
        ids = jnp.concatenate([pgot_ids(g) for g in range(groups)], axis=0)
        ids_row = jnp.sum(jnp.where(eye, ids[:, 0:1], 0.0), axis=0, keepdims=True)
        block = fiota((BLOCKS, slots), 0)
        to_own = jnp.where(block == ownr[...], 1.0, 0.0).astype(BF16)
        to_target = jnp.where(block == ids_row, 1.0, 0.0).astype(BF16)
        rh, rm = parts2(returned)
        sh, sm = parts2(second[...])
        forces[...] = (plain(to_own, rh) + plain(to_own, rm)) + (
            plain(to_target, sh) + plain(to_target, sm)
        )

    def spread(out, base):
        for part in range(2):
            for k in range(BLOCKS):
                at = slice(k * WIDTH, (k + 1) * WIDTH)
                mask = iota((256, WIDTH), 0) == map_ref[0, 0, k : k + 1, :] // DEPTH
                for c in range(3):
                    force = forces[k : k + 1, c * WIDTH : (c + 1) * WIDTH]
                    high = force.astype(BF16).astype(F32)
                    kept = high if part == 0 else force - high
                    lhs[c, part, :, at] = jnp.where(mask, kept, 0.0).astype(BF16)
        cells = jnp.concatenate([ez[k] for k in range(BLOCKS // 2)], axis=1)
        for c in range(3):
            total = lanes_t(lhs[c, 0], cells) + lanes_t(lhs[c, 1], cells)
            out[c, base : base + ROWS] = out[c, base : base + ROWS] + total.reshape(
                ROWS, COLS, DEPTH
            )

    far_count = (nb // near) * na
    place_far = (b // near) * na + a

    def peer_of(stage, other):
        if stage == 0:
            return (base_near + other, a)
        return ((other // na) * near + place_near, lax.rem(other, na))

    def ar_copy(n, stage, peer, slot):
        return pltpu.make_async_remote_copy(
            src_ref=arsend.at[n, stage], dst_ref=argot.at[n, stage, slot],
            send_sem=ar_send.at[n, stage], recv_sem=ar_recv.at[n, stage],
            device_id=peer_of(stage, peer), device_id_type=MESH,
        )

    def ar_start(n, stage, value):
        own, size = ((place_near, near), (place_far, far_count))[stage]
        arsend[n, stage] = value

        def step(t, carry):
            ar_copy(n, stage, wrap(own + t, size), own).start()
            return carry

        lax.fori_loop(1, size, step, 0)
        argot[n, stage, own] = value

    def ar_finish(n, stage):
        own, size = ((place_near, near), (place_far, far_count))[stage]

        for k in range(2):
            at = pl.ds(0, size - 1)
            arrived = pltpu.make_async_remote_copy(
                src_ref=argot.at[n, stage, at], dst_ref=argot.at[n, stage, at],
                send_sem=ar_send.at[n, stage], recv_sem=ar_recv.at[n, stage],
                device_id=peer_of(stage, wrap(own + 1, size)), device_id_type=MESH,
            )
            (arrived.wait_recv, arrived.wait_send)[k]()
        total = argot[n, stage, 0]
        for k in range(1, size):
            total = total + argot[n, stage, k]
        return total

    def rows_of(*sums):
        row = iota((8, WIDTH), 0)
        value = jnp.zeros((8, WIDTH), F32)
        for k, s in enumerate(sums):
            folded = jnp.sum(s, axis=0, keepdims=True)
            folded = sum(
                folded[:, j : j + WIDTH] for j in range(0, folded.shape[1], WIDTH)
            )
            value = jnp.where(row == k, folded, value)
        return value

    def scalar(total, k):
        return jnp.sum(total[k : k + 1], axis=1, keepdims=True)

    collect(2, rsend, rgot)
    moves1[...] = moves1[...] + forces[...]
    moves_out(3, moves1, fsend, fgot)
    spread(qx, 1)
    for c in range(3):
        ysend1[0, c] = qx[c, 1 : ROWS + 1, COLS - 1, :]
        ysend1[1, c] = qx[c, 1 : ROWS + 1, 0, :]
    halos1 = [
        halo(6, qx.at[:, last], qx.at[:, 0], (up, a)),
        halo(7, qx.at[:, 1], qx.at[:, last + 1], (down, a)),
        halo(8, ysend1.at[0], ygot1.at[0], (b, right)),
        halo(9, ysend1.at[1], ygot1.at[1], (b, left)),
    ]
    for copy in halos1:
        copy.start()
    ar_start(0, 0, rows_of(c_c, c_ec, moves0[...] * forces[...]))
    def chunk1(q):
        wait_chunk(3, fsend, fgot, q)
        for g in (2 * q, 2 * q + 1):
            mine = select3(pgot_ids(g), mparts)
            store_eight(bsend, g, sides(g, fgot, mine, False))
        send_chunk(4, bsend, bgot, q)

    q1_store = pltpu.make_async_copy(qx.at[:, pl.ds(1, ROWS)], q1_hbm, sem_out.at[0])
    q1_store.start()
    each_chunk(chunk1, -1, 0, chunks // 2)
    ar_start(0, 1, ar_finish(0, 0))
    each_chunk(chunk1, -1, chunks // 2, chunks)
    for copy in halos1:
        copy.wait_recv()
    clear_edges((qx,), ygot1)
    elastic(qx, ygot1, q2, 0, ())


    total0 = ar_finish(0, 1)
    norm0 = scalar(total0, 0)
    step0 = norm0 / (scalar(total0, 1) + scalar(total0, 2))

    def products(i, sums):
        r_r, r_ar = sums
        for c in range(3):
            q = qx[c, i + 1]
            r = cx[c, i + 1] - step0 * q
            r_r = r_r + r * r
            r_ar = r_ar + r * (q - step0 * q2[c, i])
        return r_r, r_ar

    zero = jnp.zeros((COLS, DEPTH), F32)
    r_r, r_ar = lax.fori_loop(0, ROWS, products, (zero, zero))
    collect(4, bsend, bgot)
    r_moves = moves0[...] - step0 * moves1[...]
    ar_start(1, 0, rows_of(r_r, r_ar, -step0 * (r_moves * forces[...])))
    spread(q2, 0)
    q2_store = pltpu.make_async_copy(q2, q2_hbm, sem_out.at[1])
    q2_store.start()
    ar_start(1, 1, ar_finish(1, 0))
    total1 = ar_finish(1, 1)
    norm1 = scalar(total1, 0)
    product = scalar(total1, 1) + scalar(total1, 2)
    ratio = norm1 / norm0
    step1 = norm1 / (product - ratio * norm1 / step0)
    on_first = step0 + step1 * (1.0 + ratio)
    on_second = step1 * step0

    row = iota((8, WIDTH), 0)
    coef_ref[...] = jnp.where(row == 0, on_first, on_second)
    for copy in halos0 + halos1:
        copy.wait_send()

    for phase, (src, dst) in enumerate(
        ((psend, pgot), (msend, mgot), (rsend, rgot), (fsend, fgot), (bsend, bgot))
    ):
        batch(phase, src, dst, 0, 0, nb - 1).wait_send()
    q1_store.wait()
    q2_store.wait()


def on_device(nb, na, cotangent, shear, lame, inertia, points, counts, maps, pairs):
    slots = nb * CAP
    grid = (3, ROWS, COLS, DEPTH)
    near = min(16, nb)
    peers = max(near, (nb // near) * na)

    def buffers(width):
        return [pltpu.VMEM((nb, CAP, width), F32)] * 2

    scratch = [
        pltpu.VMEM((3, ROWS + 2, COLS, DEPTH), F32),
        pltpu.VMEM((3, ROWS + 2, COLS, DEPTH), F32),
        pltpu.VMEM(grid, F32),
        pltpu.VMEM((2, ROWS + 2, COLS, DEPTH), F32),
        pltpu.VMEM((ROWS, COLS, DEPTH), F32),
        pltpu.VMEM((6, 2, ROWS, COLS, DEPTH), F32),
        pltpu.VMEM((BLOCKS // 2, DEPTH, 2 * WIDTH), BF16),
        pltpu.VMEM((768, 2 * DEPTH), BF16),
        pltpu.VMEM((3, 2, 256, BLOCKS * WIDTH), BF16),
        pltpu.VMEM((slots, 2 * WIDTH, WIDTH), BF16),
        pltpu.VMEM((BLOCKS, MOVE), F32),
        pltpu.VMEM((BLOCKS, MOVE), F32),
        pltpu.VMEM((WIDTH, MOVE), BF16),
        pltpu.VMEM((WIDTH, MOVE), BF16),
        pltpu.VMEM((slots, WIDTH), BF16),
        pltpu.VMEM((slots, WIDTH), F32),
        pltpu.VMEM((1, slots), F32),
        pltpu.VMEM((slots, MOVE), F32),
        pltpu.VMEM((slots, WIDTH), F32),
        pltpu.VMEM((slots, WIDTH), F32),
        pltpu.VMEM((BLOCKS, MOVE), F32),
        *buffers(MOVE + WIDTH),
        *buffers(MOVE),
        *buffers(MOVE),
        *buffers(MOVE),
        *buffers(MOVE),
        pltpu.VMEM((2, 5, ROWS, DEPTH), F32),
        pltpu.VMEM((2, 5, ROWS, DEPTH), F32),
        pltpu.VMEM((2, 3, ROWS, DEPTH), F32),
        pltpu.VMEM((2, 3, ROWS, DEPTH), F32),
        pltpu.VMEM((2, 2, 8, WIDTH), F32),
        pltpu.VMEM((2, 2, peers, 8, WIDTH), F32),
        pltpu.SemaphoreType.DMA((4,)),
        pltpu.SemaphoreType.DMA((2,)),
        pltpu.SemaphoreType.DMA((5,)),
        pltpu.SemaphoreType.DMA((5, nb // 4)),
        pltpu.SemaphoreType.DMA((10,)),
        pltpu.SemaphoreType.DMA((10,)),
        pltpu.SemaphoreType.DMA((2, 2)),
        pltpu.SemaphoreType.DMA((2, 2)),
    ]
    q1, q2, coef = pl.pallas_call(
        functools.partial(kernel, nb, na),
        out_shape=[jax.ShapeDtypeStruct(grid, F32)] * 2
        + [jax.ShapeDtypeStruct((8, WIDTH), F32)],
        in_specs=[pl.BlockSpec(memory_space=pl.ANY)] * 4
        + [
            pl.BlockSpec(memory_space=pltpu.VMEM),
            pl.BlockSpec(memory_space=pltpu.SMEM),
            pl.BlockSpec(memory_space=pltpu.VMEM),
            pl.BlockSpec(memory_space=pltpu.VMEM),
        ],
        out_specs=[pl.BlockSpec(memory_space=pl.ANY)] * 2
        + [pl.BlockSpec(memory_space=pltpu.VMEM)],
        scratch_shapes=scratch,
        compiler_params=pltpu.CompilerParams(
            has_side_effects=True, collective_id=0, vmem_limit_bytes=58 * 2**20
        ),
        name="adjoint_cg",
    )(
        cotangent, shear, lame, inertia,
        points[0, 0].transpose(1, 0, 2), counts, maps, pairs[0].transpose(1, 0, 2),
    )
    on_first, on_second = coef[0, 0], coef[1, 0]
    displacement = on_first * cotangent - on_second * q1
    return displacement, cotangent - on_first * q1 + on_second * q2


def solution(mesh):
    nb, na = mesh.shape["body"], mesh.shape["across"]
    split = P("body", "across")
    vector = P(None, "body", "across", None)
    return jax.shard_map(
        functools.partial(on_device, nb, na),
        mesh=mesh,
        in_specs=(vector, split, split, split, split, split, split, split),
        out_specs=(vector, vector),
        check_vma=False,
    )
```

```python
import functools

import jax
import jax.numpy as jnp
from jax import lax
from jax.experimental import pallas as pl
from jax.experimental.pallas import tpu as pltpu
from jax.sharding import PartitionSpec as P

MESH = pl.DeviceIdType.MESH
CAP = 4
ROWS, COLS, DEPTH = 8, 32, 256
BLOCKS, WIDTH = 16, 128
MOVE = 3 * WIDTH
F32, BF16 = jnp.float32, jnp.bfloat16
FAR = 100.0


def iota(shape, dim):
    return lax.broadcasted_iota(jnp.int32, shape, dim)


def fiota(shape, dim):
    return iota(shape, dim).astype(F32)


def parts2(x):
    high = x.astype(BF16)
    return high, (x - high.astype(F32)).astype(BF16)


def parts3(x):
    high = x.astype(BF16).astype(F32)
    rest = x - high
    mid = rest.astype(BF16).astype(F32)
    return high, mid, rest - mid


def lanes_t(a, b):
    return lax.dot_general(a, b, (((1,), (1,)), ((), ())), preferred_element_type=F32)


def plain(a, b):
    return jnp.dot(a, b, preferred_element_type=F32)


def kernel(
    nb, na,
    c_hbm, mu_hbm, lam_hbm, inertia_hbm, pts_ref, cnt_ref, map_ref, pair_ref,
    q1_hbm, q2_hbm, first_ref, second_ref,
    cx, qx, q2, mx, inertia, fw, ez, vhm, lhs, ws,
    moves0, moves1, mparts, pparts, own3, target3, mines, tgtc, ownr, targetr, second, rowt, colt, forces,
    psend, pgot, msend, mgot, rsend, rgot, fsend, fgot, bsend, bgot,
    ysend, ygot, ysend1, ygot1, arsend, argot,
    sem_in, sem_out, a2a_send, a2a_recv, halo_send, halo_recv, ar_send, ar_recv,
):
    b = lax.axis_index("body")
    a = lax.axis_index("across")
    slots = nb * CAP
    groups = nb // 2
    chunks = nb // 4
    me_q = b // 4

    def wrap(i, n):
        return lax.rem(i + n, n)

    near = min(16, nb)
    place_near, base_near = lax.rem(b, near), (b // near) * near
    barrier = pltpu.get_barrier_semaphore()

    def greet(peer):
        pl.semaphore_signal(barrier, inc=1, device_id=peer, device_id_type=MESH)

    def greet_body(t, carry):
        greet((wrap(b + t, nb), a))
        return carry

    lax.fori_loop(1, nb, greet_body, 0)
    for t in range(1, na):
        for k in range(nb // near):
            greet((k * near + place_near, wrap(a + t, na)))

    loads = [
        pltpu.make_async_copy(c_hbm, cx.at[:, pl.ds(1, ROWS)], sem_in.at[0]),
        pltpu.make_async_copy(mu_hbm, mx.at[0, pl.ds(1, ROWS)], sem_in.at[1]),
        pltpu.make_async_copy(lam_hbm, mx.at[1, pl.ds(1, ROWS)], sem_in.at[2]),
        pltpu.make_async_copy(inertia_hbm, inertia, sem_in.at[3]),
    ]
    for load in loads:
        load.start()

    own_row, partner_row, target_row = (pair_ref[k].astype(F32) for k in range(3))
    sub, lane = iota((slots, slots), 0), iota((slots, slots), 1)
    eye = sub == lane
    partner_col = jnp.sum(jnp.where(eye, partner_row, 0.0), axis=1, keepdims=True)
    rank = jnp.sum(
        jnp.where((partner_col == partner_row) & (sub < lane), 1.0, 0.0), axis=0, keepdims=True
    )
    slot_row = partner_row * CAP + rank
    chosen = slot_row == sub.astype(F32)
    own_col = jnp.sum(jnp.where(chosen, own_row, 0.0), axis=1, keepdims=True)
    target_col = jnp.sum(jnp.where(chosen, target_row, 0.0), axis=1, keepdims=True)
    tgtc[...] = jnp.broadcast_to(target_col, (slots, WIDTH))
    ownr[...] = jnp.sum(jnp.where(eye, own_col, 0.0), axis=0, keepdims=True)

    block_id = iota((BLOCKS, WIDTH), 0)
    count = jnp.zeros((BLOCKS, WIDTH), jnp.int32)
    for k in range(BLOCKS):
        count = jnp.where(block_id == k, cnt_ref[0, 0, k], count)
    active = iota((BLOCKS, WIDTH), 1) < count
    far = jnp.where(lax.rem(block_id, 2) == 0, FAR, -FAR)
    coords = [
        jnp.where(active, pts_ref[0] - 0.5, far),
        pts_ref[1] - 0.5,
        pts_ref[2],
    ]
    pad16 = jnp.zeros((BLOCKS, WIDTH), F32)

    def store_parts(ref, tiles):
        for c, tile in enumerate(tiles):
            stacked = jnp.concatenate([*parts3(tile)] + [pad16] * 5, axis=0)
            ref[:, c * WIDTH : (c + 1) * WIDTH] = stacked.astype(BF16)

    store_parts(pparts, coords)
    lane8 = iota((8, WIDTH), 1)
    lane3 = jnp.where(lane8 < 3 * BLOCKS, lax.rem(lane8, BLOCKS), -1).astype(F32)
    sub8 = iota((8, WIDTH), 0)

    lanes = iota((slots, WIDTH), 1)
    lanes3 = jnp.where(lanes < 3 * BLOCKS, lax.rem(lanes, BLOCKS), -1).astype(F32)
    own3[...] = jnp.where(own_col == lanes3, 1.0, 0.0).astype(BF16)

    def select3(ids, ref):
        return plain(jnp.where(ids == lane3, 1.0, 0.0).astype(BF16), ref[...])

    def eight(ref, g):
        return jnp.concatenate([ref[2 * g], ref[2 * g + 1]], axis=0)

    def store_eight(ref, g, value):
        ref[2 * g] = value[:4]
        ref[2 * g + 1] = value[4:]

    def rows8(g):
        return pl.ds(pl.multiple_of(g * 8, 8), 8)

    def a2a(phase, src, dst, peer):
        return pltpu.make_async_remote_copy(
            src_ref=src.at[peer], dst_ref=dst.at[b],
            send_sem=a2a_send.at[phase], recv_sem=a2a_recv.at[phase, arrives(phase, me_q)],
            device_id=(peer, a), device_id_type=MESH,
        )

    def arrives(phase, q):
        return 0 if phase in (2, 4) else q

    def batch(phase, src, dst, q, first, count):
        at = pl.ds(first, count)
        return pltpu.make_async_remote_copy(
            src_ref=src.at[at], dst_ref=dst.at[at],
            send_sem=a2a_send.at[phase], recv_sem=a2a_recv.at[phase, arrives(phase, q)],
            device_id=(wrap(b + 1, nb), a), device_id_type=MESH,
        )

    def send_chunk(phase, src, dst, q):
        @pl.when(q != me_q)
        def _():
            for h in range(4):
                a2a(phase, src, dst, 4 * q + h).start()

        @pl.when(q == me_q)
        def _():
            for h in range(4):
                peer = 4 * q + h

                @pl.when(peer != b)
                def _():
                    a2a(phase, src, dst, peer).start()

                @pl.when(peer == b)
                def _():
                    dst[peer] = src[peer]

    def wait_chunk(phase, src, dst, q):
        @pl.when(q != me_q)
        def _():
            batch(phase, src, dst, q, 4 * q, 4).wait_recv()

        @pl.when(q == me_q)
        def _():
            batch(phase, src, dst, q, 4 * q, 3).wait_recv()

    def each_chunk(body, sign, start=0, stop=nb // 4):
        def step(t, carry):
            body(wrap(me_q + sign * t, chunks))
            return carry

        lax.fori_loop(start, stop, step, 0)

    def store_all(ref, value):
        for k in range(nb):
            ref[k] = value[k * CAP : (k + 1) * CAP]

    store_all(psend, jnp.concatenate([plain(own3[...], pparts[...]), tgtc[...]], axis=1))
    def map_row(k):
        pair = map_ref[0, 0, pl.ds(2 * k, 1), :], map_ref[0, 0, pl.ds(2 * k + 1, 1), :]
        return jnp.concatenate(pair, axis=1)

    def place(k, carry):
        z = lax.rem(map_row(k), DEPTH)
        ez[k] = jnp.where(iota((DEPTH, 2 * WIDTH), 0) == z, 1.0, 0.0).astype(BF16)
        return carry

    lax.fori_loop(0, BLOCKS // 2, place, 0)

    pl.semaphore_wait(barrier, nb - 1 + (na - 1) * (nb // near))
    each_chunk(lambda q: send_chunk(0, psend, pgot, q), 1)
    for load in loads:
        load.wait()
    up, down = wrap(b + 1, nb), wrap(b - 1, nb)
    right, left = wrap(a + 1, na), wrap(a - 1, na)

    def halo(k, src, dst, peer):
        return pltpu.make_async_remote_copy(
            src_ref=src, dst_ref=dst, send_sem=halo_send.at[k], recv_sem=halo_recv.at[k],
            device_id=peer, device_id_type=MESH,
        )

    last = ROWS
    for c in range(3):
        ysend[0, c] = cx[c, 1 : ROWS + 1, COLS - 1, :]
        ysend[1, c] = cx[c, 1 : ROWS + 1, 0, :]
    for m in range(2):
        ysend[0, 3 + m] = mx[m, 1 : ROWS + 1, COLS - 1, :]
        ysend[1, 3 + m] = mx[m, 1 : ROWS + 1, 0, :]
    halos0 = [
        halo(0, cx.at[:, last], cx.at[:, 0], (up, a)),
        halo(1, cx.at[:, 1], cx.at[:, last + 1], (down, a)),
        halo(2, mx.at[:, last], mx.at[:, 0], (up, a)),
        halo(3, mx.at[:, 1], mx.at[:, last + 1], (down, a)),
        halo(4, ysend.at[0], ygot.at[0], (b, right)),
        halo(5, ysend.at[1], ygot.at[1], (b, left)),
    ]
    for copy in halos0:
        copy.start()

    def pick(vector, base, moves):
        for c in range(3):
            flat = vector[c, base : base + ROWS].reshape(ROWS * COLS, DEPTH)
            at = slice(c * 256, (c + 1) * 256)
            vhm[at, :DEPTH], vhm[at, DEPTH:] = parts2(flat)

        def step(k, rows):
            picked = plain(vhm[...], jnp.concatenate([ez[k], ez[k]], axis=0))
            mask = iota((256, 2 * WIDTH), 0) == map_row(k) // DEPTH
            made = []
            for c in range(3):
                kept = jnp.where(mask, picked[c * 256 : (c + 1) * 256], 0.0)
                row = jnp.sum(kept, axis=0, keepdims=True)
                lower = jnp.where(block_id == 2 * k, row[:, :WIDTH], rows[c])
                made.append(jnp.where(block_id == 2 * k + 1, row[:, WIDTH:], lower))
            return tuple(made)

        rows = lax.fori_loop(0, BLOCKS // 2, step, (pad16,) * 3)
        moves[...] = jnp.concatenate(rows, axis=1)

    pick(cx, 1, moves0)

    def tiles(value):
        return [value[:, c * WIDTH : (c + 1) * WIDTH] for c in range(3)]

    def moves_out(phase, moves, src, dst):
        store_parts(mparts, tiles(moves[...]))

        store_all(src, plain(own3[...], mparts[...]))
        each_chunk(lambda q: send_chunk(phase, src, dst, q), 1)

    moves_out(1, moves0, msend, mgot)

    row32, lane256 = iota((COLS, DEPTH), 0), iota((COLS, DEPTH), 1)

    def clear_edges(xs, yhalo):
        @pl.when(b == 0)
        def _():
            for x in xs:
                x[:, 0] = jnp.zeros_like(x[:, 0])

        @pl.when(b == nb - 1)
        def _():
            for x in xs:
                x[:, last + 1] = jnp.zeros_like(x[:, last + 1])

        @pl.when(a == 0)
        def _():
            yhalo[0] = jnp.zeros_like(yhalo[0])

        @pl.when(a == na - 1)
        def _():
            yhalo[1] = jnp.zeros_like(yhalo[1])

    def beside(v, low, high):
        return (
            jnp.where(row32 == COLS - 1, high, pltpu.roll(v, COLS - 1, 0)),
            jnp.where(row32 == 0, low, pltpu.roll(v, 1, 0)),
            jnp.where(lane256 == DEPTH - 1, 0.0, pltpu.roll(v, DEPTH - 1, 1)),
            jnp.where(lane256 == 0, 0.0, pltpu.roll(v, 1, 1)),
        )

    def faces(i, carry):
        mu, lam = mx[0, i + 1], mx[1, i + 1]
        near_mu = (mx[0, i + 2], mx[0, i]) + beside(
            mu, ygot[0, 3, pl.ds(i, 1), :], ygot[1, 3, pl.ds(i, 1), :]
        )
        near_lam = (mx[1, i + 2], mx[1, i]) + beside(
            lam, ygot[0, 4, pl.ds(i, 1), :], ygot[1, 4, pl.ds(i, 1), :]
        )
        cut = nb // 4
        open_high = jnp.where((b == cut - 1) & (i == ROWS - 1), 0.0, 0.5)
        open_low = jnp.where((b == cut) & (i == 0), 0.0, 0.5)
        for k in range(6):
            half = (open_high, open_low, 0.5, 0.5, 0.5, 0.5)[k]
            plain_weight = half * (mu + near_mu[k])
            fw[k, 0, i] = plain_weight
            fw[k, 1, i] = 2.0 * plain_weight + half * (lam + near_lam[k])
        return carry

    def elastic(vector, yhalo, out, base, others):
        def plane(i, sums):
            sums = list(sums)
            for c in range(3):
                v = vector[c, i + 1]
                near = (vector[c, i + 2], vector[c, i]) + beside(
                    v, yhalo[0, c, pl.ds(i, 1), :], yhalo[1, c, pl.ds(i, 1), :]
                )
                value = inertia[i] * v
                for k in range(6):
                    value = value + fw[k, int(k // 2 == c), i] * (v - near[k])
                out[c, base + i] = value
                for n, other in enumerate(others):
                    sums[n] = sums[n] + value * other[c, i + 1]
            return tuple(sums)

        zero = jnp.zeros((COLS, DEPTH), F32)
        return lax.fori_loop(0, ROWS, plane, (zero,) * len(others))

    ones8 = jnp.ones((8, WIDTH), F32)

    def weigh(g):
        got = eight(pgot, g)
        ids = got[:, MOVE:]
        picked = jnp.where(ids == lane3, 1.0, 0.0).astype(BF16)
        picked = plain(picked, jnp.concatenate([pparts[...], mparts[...]], axis=1))
        ys, mine = tiles(picked), picked[:, MOVE:]
        made = []
        pad = jnp.zeros((WIDTH - 24, WIDTH), F32)
        xs = jnp.concatenate(tiles(got) + [pad], axis=0).T
        for r in range(8):
            squared = None
            for c in range(3):
                apart = xs[:, 8 * c + r : 8 * c + r + 1] - ys[c][r : r + 1]
                squared = apart * apart if squared is None else squared + apart * apart
            squared = jnp.minimum(squared, 1.0)
            inverse = 1.0 / squared
            weight = 0.005 * (inverse * (inverse + 2.0) - 3.0) - 0.01 * jnp.log(squared)
            made.append(jnp.concatenate(parts2(weight), axis=0))
            ws[g * 8 + r] = made[r]
        return made, mine

    def halves(value, extra):
        rows = []
        for tile in tiles(value):
            high = tile.astype(BF16).astype(F32)
            rows += [high, tile - high]
        return rows + extra

    def only(rows, keep):
        kept = [jnp.where(keep, row, 0.0) for row in rows]
        return jnp.concatenate(kept, axis=0).astype(BF16)

    def sides(g, dst, w, mine, first_phase):
        got = eight(dst, g)
        extra = [ones8, ones8] if first_phase else []
        v_rows, u_rows = halves(got, extra), halves(mine, extra)
        v_side, w_side = [], []
        for q in range(4):
            kept = only(v_rows, lax.rem(sub8, 4) == q)
            v_side += [kept, kept]
            w_side.append(jnp.concatenate([w[q], w[q + 4]], axis=1))
        to_second = plain(jnp.concatenate(v_side, axis=1), jnp.concatenate(w_side, axis=0))
        u_side = jnp.concatenate([only(u_rows, sub8 == r) for r in range(8)], axis=1)
        to_first = lanes_t(u_side, jnp.concatenate(w, axis=1))
        to_first = to_first[:, :WIDTH] + to_first[:, WIDTH:]
        into_second, into_first = [], []
        for k in range(len(v_rows)):
            at = slice(8 * k, 8 * k + 8)
            into_second.append(
                jnp.where(sub8 < 4, to_second[at, :WIDTH], to_second[at, WIDTH:])
            )
            into_first.append(to_first[at])
        at = rows8(g)
        if first_phase:
            rowt[at], colt[at] = into_first[6], into_second[6]
        row_total, col_total = rowt[at], colt[at]

        def force(move, total, parts, c):
            return move * total - (parts[2 * c] + parts[2 * c + 1])

        second[at] = jnp.concatenate(
            [force(u, col_total, into_second, c) for c, u in enumerate(tiles(mine))], axis=1
        )
        return jnp.concatenate(
            [force(v, row_total, into_first, c) for c, v in enumerate(tiles(got))], axis=1
        )

    def pgot_ids(g):
        return jnp.concatenate([pgot[2 * g, :, MOVE:], pgot[2 * g + 1, :, MOVE:]], axis=0)

    def chunk0(q):
        wait_chunk(0, psend, pgot, q)
        wait_chunk(1, msend, mgot, q)
        weighed = [weigh(g) for g in (2 * q, 2 * q + 1)]
        made = [sides(2 * q + k, mgot, *weighed[k], True) for k in range(2)]
        for k in range(2):
            store_eight(rsend, 2 * q + k, made[k])
        send_chunk(2, rsend, rgot, q)

    each_chunk(chunk0, -1)

    for copy in halos0:
        copy.wait_recv()
    clear_edges((cx, mx), ygot)
    lax.fori_loop(0, ROWS, faces, 0)
    (c_ec,) = elastic(cx, ygot, qx, 1, (cx,))
    pick(qx, 1, moves1)
    c_c = jnp.zeros((COLS, DEPTH), F32)
    for c in range(3):
        for i in range(ROWS):
            c_c = c_c + cx[c, i + 1] * cx[c, i + 1]


    def note_targets():
        ids = jnp.concatenate([pgot_ids(g) for g in range(groups)], axis=0)
        target3[...] = jnp.where(ids == lanes3, 1.0, 0.0).astype(BF16)
        targetr[...] = jnp.sum(jnp.where(eye, ids[:, 0:1], 0.0), axis=0, keepdims=True)

    def collect(phase, src, dst):
        batch(phase, src, dst, 0, 0, nb - 1).wait_recv()
        returned = jnp.concatenate([eight(dst, g) for g in range(groups)], axis=0)
        block = fiota((BLOCKS, slots), 0)
        to_own = jnp.where(block == ownr[...], 1.0, 0.0).astype(BF16)
        to_target = jnp.where(block == targetr[...], 1.0, 0.0).astype(BF16)
        rh, rm = parts2(returned)
        sh, sm = parts2(second[...])
        forces[...] = (plain(to_own, rh) + plain(to_own, rm)) + (
            plain(to_target, sh) + plain(to_target, sm)
        )

    def spread(out, base):
        for part in range(2):
            for k in range(BLOCKS):
                at = slice(k * WIDTH, (k + 1) * WIDTH)
                mask = iota((256, WIDTH), 0) == map_ref[0, 0, k : k + 1, :] // DEPTH
                for c in range(3):
                    force = forces[k : k + 1, c * WIDTH : (c + 1) * WIDTH]
                    high = force.astype(BF16).astype(F32)
                    kept = high if part == 0 else force - high
                    lhs[c, part, :, at] = jnp.where(mask, kept, 0.0).astype(BF16)
        cells = jnp.concatenate([ez[k] for k in range(BLOCKS // 2)], axis=1)
        for c in range(3):
            total = lanes_t(lhs[c, 0], cells) + lanes_t(lhs[c, 1], cells)
            out[c, base : base + ROWS] = out[c, base : base + ROWS] + total.reshape(
                ROWS, COLS, DEPTH
            )

    far_count = (nb // near) * na
    place_far = (b // near) * na + a

    def peer_of(stage, other):
        if stage == 0:
            return (base_near + other, a)
        return ((other // na) * near + place_near, lax.rem(other, na))

    def ar_copy(n, stage, peer, slot):
        return pltpu.make_async_remote_copy(
            src_ref=arsend.at[n, stage], dst_ref=argot.at[n, stage, slot],
            send_sem=ar_send.at[n, stage], recv_sem=ar_recv.at[n, stage],
            device_id=peer_of(stage, peer), device_id_type=MESH,
        )

    def ar_start(n, stage, value):
        own, size = ((place_near, near), (place_far, far_count))[stage]
        arsend[n, stage] = value

        def step(t, carry):
            ar_copy(n, stage, wrap(own + t, size), own).start()
            return carry

        lax.fori_loop(1, size, step, 0)
        argot[n, stage, own] = value

    def ar_finish(n, stage):
        own, size = ((place_near, near), (place_far, far_count))[stage]

        for k in range(2):
            at = pl.ds(0, size - 1)
            arrived = pltpu.make_async_remote_copy(
                src_ref=argot.at[n, stage, at], dst_ref=argot.at[n, stage, at],
                send_sem=ar_send.at[n, stage], recv_sem=ar_recv.at[n, stage],
                device_id=peer_of(stage, wrap(own + 1, size)), device_id_type=MESH,
            )
            (arrived.wait_recv, arrived.wait_send)[k]()
        total = argot[n, stage, 0]
        for k in range(1, size):
            total = total + argot[n, stage, k]
        return total

    def rows_of(*sums):
        row = iota((8, WIDTH), 0)
        value = jnp.zeros((8, WIDTH), F32)
        for k, s in enumerate(sums):
            folded = jnp.sum(s, axis=0, keepdims=True)
            folded = sum(
                folded[:, j : j + WIDTH] for j in range(0, folded.shape[1], WIDTH)
            )
            value = jnp.where(row == k, folded, value)
        return value

    def scalar(total, k):
        return jnp.sum(total[k : k + 1], axis=1, keepdims=True)

    note_targets()
    collect(2, rsend, rgot)
    moves1[...] = moves1[...] + forces[...]
    moves_out(3, moves1, fsend, fgot)
    mines[...] = plain(target3[...], mparts[...])
    spread(qx, 1)
    for c in range(3):
        ysend1[0, c] = qx[c, 1 : ROWS + 1, COLS - 1, :]
        ysend1[1, c] = qx[c, 1 : ROWS + 1, 0, :]
    halos1 = [
        halo(6, qx.at[:, last], qx.at[:, 0], (up, a)),
        halo(7, qx.at[:, 1], qx.at[:, last + 1], (down, a)),
        halo(8, ysend1.at[0], ygot1.at[0], (b, right)),
        halo(9, ysend1.at[1], ygot1.at[1], (b, left)),
    ]
    for copy in halos1:
        copy.start()
    ar_start(0, 0, rows_of(c_c, c_ec, moves0[...] * forces[...]))
    def chunk1(q):
        wait_chunk(3, fsend, fgot, q)
        made = []
        for g in (2 * q, 2 * q + 1):
            w = [ws[g * 8 + r] for r in range(8)]
            made.append(sides(g, fgot, w, mines[rows8(g)], False))
        for k in range(2):
            store_eight(bsend, 2 * q + k, made[k])
        send_chunk(4, bsend, bgot, q)

    q1_store = pltpu.make_async_copy(qx.at[:, pl.ds(1, ROWS)], q1_hbm, sem_out.at[0])
    q1_store.start()
    each_chunk(chunk1, -1, 0, chunks // 2)
    ar_start(0, 1, ar_finish(0, 0))
    each_chunk(chunk1, -1, chunks // 2, chunks)
    for copy in halos1:
        copy.wait_recv()
    clear_edges((qx,), ygot1)
    elastic(qx, ygot1, q2, 0, ())


    total0 = ar_finish(0, 1)
    norm0 = scalar(total0, 0)
    step0 = norm0 / (scalar(total0, 1) + scalar(total0, 2))

    def products(i, sums):
        r_r, r_ar = sums
        for c in range(3):
            q = qx[c, i + 1]
            r = cx[c, i + 1] - step0 * q
            r_r = r_r + r * r
            r_ar = r_ar + r * (q - step0 * q2[c, i])
        return r_r, r_ar

    zero = jnp.zeros((COLS, DEPTH), F32)
    r_r, r_ar = lax.fori_loop(0, ROWS, products, (zero, zero))
    collect(4, bsend, bgot)
    r_moves = moves0[...] - step0 * moves1[...]
    ar_start(1, 0, rows_of(r_r, r_ar, -step0 * (r_moves * forces[...])))
    spread(q2, 0)
    q2_store = pltpu.make_async_copy(q2, q2_hbm, sem_out.at[1])
    q2_store.start()
    ar_start(1, 1, ar_finish(1, 0))
    total1 = ar_finish(1, 1)
    norm1 = scalar(total1, 0)
    product = scalar(total1, 1) + scalar(total1, 2)
    ratio = norm1 / norm0
    step1 = norm1 / (product - ratio * norm1 / step0)
    on_first = step0 + step1 * (1.0 + ratio)
    on_second = step1 * step0

    first_ref[0] = on_first[0, 0]
    second_ref[0] = on_second[0, 0]
    for copy in halos0 + halos1:
        copy.wait_send()

    for phase, (src, dst) in enumerate(
        ((psend, pgot), (msend, mgot), (rsend, rgot), (fsend, fgot), (bsend, bgot))
    ):
        batch(phase, src, dst, 0, 0, nb - 1).wait_send()
    q1_store.wait()
    q2_store.wait()


def combine(first_ref, second_ref, c_ref, q1_ref, q2_ref, disp_ref, res_ref):
    on_first, on_second = first_ref[0], second_ref[0]
    disp_ref[...] = on_first * c_ref[...] - on_second * q1_ref[...]
    res_ref[...] = c_ref[...] - on_first * q1_ref[...] + on_second * q2_ref[...]


def on_device(nb, na, cotangent, shear, lame, inertia, points, counts, maps, pairs):
    slots = nb * CAP
    grid = (3, ROWS, COLS, DEPTH)
    near = min(16, nb)
    peers = max(near, (nb // near) * na)

    def buffers(width):
        return [pltpu.VMEM((nb, CAP, width), F32)] * 2

    scratch = [
        pltpu.VMEM((3, ROWS + 2, COLS, DEPTH), F32),
        pltpu.VMEM((3, ROWS + 2, COLS, DEPTH), F32),
        pltpu.VMEM(grid, F32),
        pltpu.VMEM((2, ROWS + 2, COLS, DEPTH), F32),
        pltpu.VMEM((ROWS, COLS, DEPTH), F32),
        pltpu.VMEM((6, 2, ROWS, COLS, DEPTH), F32),
        pltpu.VMEM((BLOCKS // 2, DEPTH, 2 * WIDTH), BF16),
        pltpu.VMEM((768, 2 * DEPTH), BF16),
        pltpu.VMEM((3, 2, 256, BLOCKS * WIDTH), BF16),
        pltpu.VMEM((slots, 2 * WIDTH, WIDTH), BF16),
        pltpu.VMEM((BLOCKS, MOVE), F32),
        pltpu.VMEM((BLOCKS, MOVE), F32),
        pltpu.VMEM((WIDTH, MOVE), BF16),
        pltpu.VMEM((WIDTH, MOVE), BF16),
        pltpu.VMEM((slots, WIDTH), BF16),
        pltpu.VMEM((slots, WIDTH), BF16),
        pltpu.VMEM((slots, MOVE), F32),
        pltpu.VMEM((slots, WIDTH), F32),
        pltpu.VMEM((1, slots), F32),
        pltpu.VMEM((1, slots), F32),
        pltpu.VMEM((slots, MOVE), F32),
        pltpu.VMEM((slots, WIDTH), F32),
        pltpu.VMEM((slots, WIDTH), F32),
        pltpu.VMEM((BLOCKS, MOVE), F32),
        *buffers(MOVE + WIDTH),
        *buffers(MOVE),
        *buffers(MOVE),
        *buffers(MOVE),
        *buffers(MOVE),
        pltpu.VMEM((2, 5, ROWS, DEPTH), F32),
        pltpu.VMEM((2, 5, ROWS, DEPTH), F32),
        pltpu.VMEM((2, 3, ROWS, DEPTH), F32),
        pltpu.VMEM((2, 3, ROWS, DEPTH), F32),
        pltpu.VMEM((2, 2, 8, WIDTH), F32),
        pltpu.VMEM((2, 2, peers, 8, WIDTH), F32),
        pltpu.SemaphoreType.DMA((4,)),
        pltpu.SemaphoreType.DMA((2,)),
        pltpu.SemaphoreType.DMA((5,)),
        pltpu.SemaphoreType.DMA((5, nb // 4)),
        pltpu.SemaphoreType.DMA((10,)),
        pltpu.SemaphoreType.DMA((10,)),
        pltpu.SemaphoreType.DMA((2, 2)),
        pltpu.SemaphoreType.DMA((2, 2)),
    ]
    q1, q2, on_first, on_second = pl.pallas_call(
        functools.partial(kernel, nb, na),
        out_shape=[jax.ShapeDtypeStruct(grid, F32)] * 2
        + [jax.ShapeDtypeStruct((1,), F32)] * 2,
        in_specs=[pl.BlockSpec(memory_space=pl.ANY)] * 4
        + [
            pl.BlockSpec(memory_space=pltpu.VMEM),
            pl.BlockSpec(memory_space=pltpu.SMEM),
            pl.BlockSpec(memory_space=pltpu.VMEM),
            pl.BlockSpec(memory_space=pltpu.VMEM),
        ],
        out_specs=[pl.BlockSpec(memory_space=pl.ANY)] * 2
        + [pl.BlockSpec(memory_space=pltpu.SMEM)] * 2,
        scratch_shapes=scratch,
        compiler_params=pltpu.CompilerParams(
            has_side_effects=True, collective_id=0, vmem_limit_bytes=58 * 2**20
        ),
        name="adjoint_cg",
    )(
        cotangent, shear, lame, inertia,
        points[0, 0].transpose(1, 0, 2), counts, maps, pairs[0].transpose(1, 0, 2),
    )
    part = pl.BlockSpec((3, 2, COLS, DEPTH), lambda i: (0, i, 0, 0))
    number = pl.BlockSpec(memory_space=pltpu.SMEM)
    return pl.pallas_call(
        combine,
        grid=(ROWS // 2,),
        out_shape=[jax.ShapeDtypeStruct(grid, F32)] * 2,
        in_specs=[number, number, part, part, part],
        out_specs=[part, part],
        name="combine",
    )(on_first, on_second, cotangent, q1, q2)


def solution(mesh):
    nb, na = mesh.shape["body"], mesh.shape["across"]
    split = P("body", "across")
    vector = P(None, "body", "across", None)
    return jax.shard_map(
        functools.partial(on_device, nb, na),
        mesh=mesh,
        in_specs=(vector, split, split, split, split, split, split, split),
        out_specs=(vector, vector),
        check_vma=False,
    )
```

```python
import functools

import jax
import jax.numpy as jnp
from jax import lax
from jax.experimental import pallas as pl
from jax.experimental.pallas import tpu as pltpu
from jax.sharding import PartitionSpec as P

MESH = pl.DeviceIdType.MESH
CAP = 4
ROWS, COLS, DEPTH = 8, 32, 256
BLOCKS, WIDTH = 16, 128
MOVE = 3 * WIDTH
F32, BF16 = jnp.float32, jnp.bfloat16
FAR = 100.0


def iota(shape, dim):
    return lax.broadcasted_iota(jnp.int32, shape, dim)


def fiota(shape, dim):
    return iota(shape, dim).astype(F32)


def parts2(x):
    high = x.astype(BF16)
    return high, (x - high.astype(F32)).astype(BF16)


def parts3(x):
    high = x.astype(BF16).astype(F32)
    rest = x - high
    mid = rest.astype(BF16).astype(F32)
    return high, mid, rest - mid


def lanes_t(a, b):
    return lax.dot_general(a, b, (((1,), (1,)), ((), ())), preferred_element_type=F32)


def plain(a, b):
    return jnp.dot(a, b, preferred_element_type=F32)


def kernel(
    nb, na,
    c_hbm, mu_hbm, lam_hbm, inertia_hbm, pts_ref, cnt_ref, map_ref, pair_ref,
    disp_ref, res_ref,
    cx, qx, q2, mx, inertia, fw, ez, vhm, lhs, ws,
    moves0, moves1, mparts, pparts, own3, target3, mines, tgtc, ownr, targetr, second, rowt, colt, forces,
    psend, pgot, rsend, rgot, fsend, fgot, bsend, bgot,
    ysend, ygot, ysend1, ygot1, arsend, argot,
    sem_in, a2a_send, a2a_recv, halo_send, halo_recv, ar_send, ar_recv,
):
    b = lax.axis_index("body")
    a = lax.axis_index("across")
    slots = nb * CAP
    groups = nb // 2
    chunks = nb // 4
    me_q = b // 4

    def wrap(i, n):
        return lax.rem(i + n, n)

    near = min(16, nb)
    place_near, base_near = lax.rem(b, near), (b // near) * near
    barrier = pltpu.get_barrier_semaphore()

    def greet(peer):
        pl.semaphore_signal(barrier, inc=1, device_id=peer, device_id_type=MESH)

    def greet_body(t, carry):
        greet((wrap(b + t, nb), a))
        return carry

    lax.fori_loop(1, nb, greet_body, 0)
    for t in range(1, na):
        for k in range(nb // near):
            greet((k * near + place_near, wrap(a + t, na)))

    loads = [
        pltpu.make_async_copy(c_hbm, cx.at[:, pl.ds(1, ROWS)], sem_in.at[0]),
        pltpu.make_async_copy(mu_hbm, mx.at[0, pl.ds(1, ROWS)], sem_in.at[1]),
        pltpu.make_async_copy(lam_hbm, mx.at[1, pl.ds(1, ROWS)], sem_in.at[2]),
        pltpu.make_async_copy(inertia_hbm, inertia, sem_in.at[3]),
    ]
    for load in loads:
        load.start()

    own_row, partner_row, target_row = (pair_ref[k].astype(F32) for k in range(3))
    sub, lane = iota((slots, slots), 0), iota((slots, slots), 1)
    eye = sub == lane
    partner_col = jnp.sum(jnp.where(eye, partner_row, 0.0), axis=1, keepdims=True)
    rank = jnp.sum(
        jnp.where((partner_col == partner_row) & (sub < lane), 1.0, 0.0), axis=0, keepdims=True
    )
    slot_row = partner_row * CAP + rank
    chosen = slot_row == sub.astype(F32)
    own_col = jnp.sum(jnp.where(chosen, own_row, 0.0), axis=1, keepdims=True)
    target_col = jnp.sum(jnp.where(chosen, target_row, 0.0), axis=1, keepdims=True)
    tgtc[...] = jnp.broadcast_to(target_col, (slots, WIDTH))
    ownr[...] = jnp.sum(jnp.where(eye, own_col, 0.0), axis=0, keepdims=True)

    block_id = iota((BLOCKS, WIDTH), 0)
    count = jnp.zeros((BLOCKS, WIDTH), jnp.int32)
    for k in range(BLOCKS):
        count = jnp.where(block_id == k, cnt_ref[0, 0, k], count)
    active = iota((BLOCKS, WIDTH), 1) < count
    far = jnp.where(lax.rem(block_id, 2) == 0, FAR, -FAR)
    coords = [
        jnp.where(active, pts_ref[0] - 0.5, far),
        pts_ref[1] - 0.5,
        pts_ref[2],
    ]
    pad16 = jnp.zeros((BLOCKS, WIDTH), F32)

    def store_parts(ref, tiles):
        for c, tile in enumerate(tiles):
            stacked = jnp.concatenate([*parts3(tile)] + [pad16] * 5, axis=0)
            ref[:, c * WIDTH : (c + 1) * WIDTH] = stacked.astype(BF16)

    store_parts(pparts, coords)
    lane8 = iota((8, WIDTH), 1)
    lane3 = jnp.where(lane8 < 3 * BLOCKS, lax.rem(lane8, BLOCKS), -1).astype(F32)
    sub8 = iota((8, WIDTH), 0)

    lanes = iota((slots, WIDTH), 1)
    lanes3 = jnp.where(lanes < 3 * BLOCKS, lax.rem(lanes, BLOCKS), -1).astype(F32)
    own3[...] = jnp.where(own_col == lanes3, 1.0, 0.0).astype(BF16)

    def select3(ids, ref):
        return plain(jnp.where(ids == lane3, 1.0, 0.0).astype(BF16), ref[...])

    def eight(ref, g):
        return jnp.concatenate([ref[2 * g], ref[2 * g + 1]], axis=0)

    def store_eight(ref, g, value):
        ref[2 * g] = value[:4]
        ref[2 * g + 1] = value[4:]

    def rows8(g):
        return pl.ds(pl.multiple_of(g * 8, 8), 8)

    def a2a(phase, src, dst, peer):
        return pltpu.make_async_remote_copy(
            src_ref=src.at[peer], dst_ref=dst.at[b],
            send_sem=a2a_send.at[phase], recv_sem=a2a_recv.at[phase, arrives(phase, me_q)],
            device_id=(peer, a), device_id_type=MESH,
        )

    def arrives(phase, q):
        return 0 if phase in (2, 4) else q

    def batch(phase, src, dst, q, first, count):
        at = pl.ds(first, count)
        return pltpu.make_async_remote_copy(
            src_ref=src.at[at], dst_ref=dst.at[at],
            send_sem=a2a_send.at[phase], recv_sem=a2a_recv.at[phase, arrives(phase, q)],
            device_id=(wrap(b + 1, nb), a), device_id_type=MESH,
        )

    def send_chunk(phase, src, dst, q):
        @pl.when(q != me_q)
        def _():
            for h in range(4):
                a2a(phase, src, dst, 4 * q + h).start()

        @pl.when(q == me_q)
        def _():
            for h in range(4):
                peer = 4 * q + h

                @pl.when(peer != b)
                def _():
                    a2a(phase, src, dst, peer).start()

                @pl.when(peer == b)
                def _():
                    dst[peer] = src[peer]

    def wait_chunk(phase, src, dst, q):
        @pl.when(q != me_q)
        def _():
            batch(phase, src, dst, q, 4 * q, 4).wait_recv()

        @pl.when(q == me_q)
        def _():
            batch(phase, src, dst, q, 4 * q, 3).wait_recv()

    def each_chunk(body, sign, start=0, stop=nb // 4):
        def step(t, carry):
            body(wrap(me_q + sign * t, chunks))
            return carry

        lax.fori_loop(start, stop, step, 0)

    def store_all(ref, value):
        for k in range(nb):
            ref[k] = value[k * CAP : (k + 1) * CAP]

    def map_row(k):
        pair = map_ref[0, 0, pl.ds(2 * k, 1), :], map_ref[0, 0, pl.ds(2 * k + 1, 1), :]
        return jnp.concatenate(pair, axis=1)

    def place(k, carry):
        z = lax.rem(map_row(k), DEPTH)
        ez[k] = jnp.where(iota((DEPTH, 2 * WIDTH), 0) == z, 1.0, 0.0).astype(BF16)
        return carry

    lax.fori_loop(0, BLOCKS // 2, place, 0)

    def pick(vector, base, moves):
        for c in range(3):
            flat = vector[c, base : base + ROWS].reshape(ROWS * COLS, DEPTH)
            at = slice(c * 256, (c + 1) * 256)
            vhm[at, :DEPTH], vhm[at, DEPTH:] = parts2(flat)

        def step(k, rows):
            picked = plain(vhm[...], jnp.concatenate([ez[k], ez[k]], axis=0))
            mask = iota((256, 2 * WIDTH), 0) == map_row(k) // DEPTH
            made = []
            for c in range(3):
                kept = jnp.where(mask, picked[c * 256 : (c + 1) * 256], 0.0)
                row = jnp.sum(kept, axis=0, keepdims=True)
                lower = jnp.where(block_id == 2 * k, row[:, :WIDTH], rows[c])
                made.append(jnp.where(block_id == 2 * k + 1, row[:, WIDTH:], lower))
            return tuple(made)

        rows = lax.fori_loop(0, BLOCKS // 2, step, (pad16,) * 3)
        moves[...] = jnp.concatenate(rows, axis=1)

    for load in loads:
        load.wait()
    pick(cx, 1, moves0)

    def tiles(value):
        return [value[:, c * WIDTH : (c + 1) * WIDTH] for c in range(3)]

    def moves_out(phase, moves, src, dst):
        store_parts(mparts, tiles(moves[...]))

        store_all(src, plain(own3[...], mparts[...]))
        each_chunk(lambda q: send_chunk(phase, src, dst, q), 1)

    store_parts(mparts, tiles(moves0[...]))
    first = [plain(own3[...], pparts[...]), tgtc[...], plain(own3[...], mparts[...])]
    store_all(psend, jnp.concatenate(first, axis=1))

    up, down = wrap(b + 1, nb), wrap(b - 1, nb)
    right, left = wrap(a + 1, na), wrap(a - 1, na)

    def halo(k, src, dst, peer):
        return pltpu.make_async_remote_copy(
            src_ref=src, dst_ref=dst, send_sem=halo_send.at[k], recv_sem=halo_recv.at[k],
            device_id=peer, device_id_type=MESH,
        )

    last = ROWS
    for c in range(3):
        ysend[0, c] = cx[c, 1 : ROWS + 1, COLS - 1, :]
        ysend[1, c] = cx[c, 1 : ROWS + 1, 0, :]
    for m in range(2):
        ysend[0, 3 + m] = mx[m, 1 : ROWS + 1, COLS - 1, :]
        ysend[1, 3 + m] = mx[m, 1 : ROWS + 1, 0, :]
    halos0 = [
        halo(0, cx.at[:, last], cx.at[:, 0], (up, a)),
        halo(1, cx.at[:, 1], cx.at[:, last + 1], (down, a)),
        halo(2, mx.at[:, last], mx.at[:, 0], (up, a)),
        halo(3, mx.at[:, 1], mx.at[:, last + 1], (down, a)),
        halo(4, ysend.at[0], ygot.at[0], (b, right)),
        halo(5, ysend.at[1], ygot.at[1], (b, left)),
    ]
    pl.semaphore_wait(barrier, nb - 1 + (na - 1) * (nb // near))
    each_chunk(lambda q: send_chunk(0, psend, pgot, q), 1)
    for copy in halos0:
        copy.start()

    row32, lane256 = iota((COLS, DEPTH), 0), iota((COLS, DEPTH), 1)

    def clear_edges(xs, yhalo):
        @pl.when(b == 0)
        def _():
            for x in xs:
                x[:, 0] = jnp.zeros_like(x[:, 0])

        @pl.when(b == nb - 1)
        def _():
            for x in xs:
                x[:, last + 1] = jnp.zeros_like(x[:, last + 1])

        @pl.when(a == 0)
        def _():
            yhalo[0] = jnp.zeros_like(yhalo[0])

        @pl.when(a == na - 1)
        def _():
            yhalo[1] = jnp.zeros_like(yhalo[1])

    def beside(v, low, high):
        return (
            jnp.where(row32 == COLS - 1, high, pltpu.roll(v, COLS - 1, 0)),
            jnp.where(row32 == 0, low, pltpu.roll(v, 1, 0)),
            jnp.where(lane256 == DEPTH - 1, 0.0, pltpu.roll(v, DEPTH - 1, 1)),
            jnp.where(lane256 == 0, 0.0, pltpu.roll(v, 1, 1)),
        )

    def faces(i, carry):
        mu, lam = mx[0, i + 1], mx[1, i + 1]
        near_mu = (mx[0, i + 2], mx[0, i]) + beside(
            mu, ygot[0, 3, pl.ds(i, 1), :], ygot[1, 3, pl.ds(i, 1), :]
        )
        near_lam = (mx[1, i + 2], mx[1, i]) + beside(
            lam, ygot[0, 4, pl.ds(i, 1), :], ygot[1, 4, pl.ds(i, 1), :]
        )
        cut = nb // 4
        open_high = jnp.where((b == cut - 1) & (i == ROWS - 1), 0.0, 0.5)
        open_low = jnp.where((b == cut) & (i == 0), 0.0, 0.5)
        for k in range(6):
            half = (open_high, open_low, 0.5, 0.5, 0.5, 0.5)[k]
            plain_weight = half * (mu + near_mu[k])
            fw[k, 0, i] = plain_weight
            fw[k, 1, i] = 2.0 * plain_weight + half * (lam + near_lam[k])
        return carry

    def elastic(vector, yhalo, out, base, others):
        def plane(i, sums):
            sums = list(sums)
            for c in range(3):
                v = vector[c, i + 1]
                near = (vector[c, i + 2], vector[c, i]) + beside(
                    v, yhalo[0, c, pl.ds(i, 1), :], yhalo[1, c, pl.ds(i, 1), :]
                )
                value = inertia[i] * v
                for k in range(6):
                    value = value + fw[k, int(k // 2 == c), i] * (v - near[k])
                out[c, base + i] = value
                for n, other in enumerate(others):
                    sums[n] = sums[n] + value * other[c, i + 1]
            return tuple(sums)

        zero = jnp.zeros((COLS, DEPTH), F32)
        return lax.fori_loop(0, ROWS, plane, (zero,) * len(others))

    ones8 = jnp.ones((8, WIDTH), F32)

    def weigh(g):
        got = eight(pgot, g)
        ids = got[:, MOVE : MOVE + WIDTH]
        picked = jnp.where(ids == lane3, 1.0, 0.0).astype(BF16)
        picked = plain(picked, jnp.concatenate([pparts[...], mparts[...]], axis=1))
        ys, mine = tiles(picked), picked[:, MOVE:]
        made = []
        pad = jnp.zeros((WIDTH - 24, WIDTH), F32)
        xs = jnp.concatenate(tiles(got) + [pad], axis=0).T
        for r in range(8):
            squared = None
            for c in range(3):
                apart = xs[:, 8 * c + r : 8 * c + r + 1] - ys[c][r : r + 1]
                squared = apart * apart if squared is None else squared + apart * apart
            squared = jnp.minimum(squared, 1.0)
            inverse = 1.0 / squared
            weight = 0.005 * (inverse * (inverse + 2.0) - 3.0) - 0.01 * jnp.log(squared)
            made.append(jnp.concatenate(parts2(weight), axis=0))
            ws[g * 8 + r] = made[r]
        return got[:, MOVE + WIDTH :], made, mine

    def halves(value, extra):
        rows = []
        for tile in tiles(value):
            high = tile.astype(BF16).astype(F32)
            rows += [high, tile - high]
        return rows + extra

    def only(rows, keep):
        kept = [jnp.where(keep, row, 0.0) for row in rows]
        return jnp.concatenate(kept, axis=0).astype(BF16)

    def sides(g, got, w, mine, first_phase):
        extra = [ones8, ones8] if first_phase else []
        v_rows, u_rows = halves(got, extra), halves(mine, extra)
        v_side, w_side = [], []
        for q in range(4):
            kept = only(v_rows, lax.rem(sub8, 4) == q)
            v_side += [kept, kept]
            w_side.append(jnp.concatenate([w[q], w[q + 4]], axis=1))
        to_second = plain(jnp.concatenate(v_side, axis=1), jnp.concatenate(w_side, axis=0))
        u_side = jnp.concatenate([only(u_rows, sub8 == r) for r in range(8)], axis=1)
        to_first = lanes_t(u_side, jnp.concatenate(w, axis=1))
        to_first = to_first[:, :WIDTH] + to_first[:, WIDTH:]
        into_second, into_first = [], []
        for k in range(len(v_rows)):
            at = slice(8 * k, 8 * k + 8)
            into_second.append(
                jnp.where(sub8 < 4, to_second[at, :WIDTH], to_second[at, WIDTH:])
            )
            into_first.append(to_first[at])
        at = rows8(g)
        if first_phase:
            rowt[at], colt[at] = into_first[6], into_second[6]
        row_total, col_total = rowt[at], colt[at]

        def force(move, total, parts, c):
            return move * total - (parts[2 * c] + parts[2 * c + 1])

        second[at] = jnp.concatenate(
            [force(u, col_total, into_second, c) for c, u in enumerate(tiles(mine))], axis=1
        )
        return jnp.concatenate(
            [force(v, row_total, into_first, c) for c, v in enumerate(tiles(got))], axis=1
        )

    def pgot_ids(g):
        return jnp.concatenate([pgot[2 * g, :, MOVE : MOVE + WIDTH], pgot[2 * g + 1, :, MOVE : MOVE + WIDTH]], axis=0)

    def chunk0(q):
        wait_chunk(0, psend, pgot, q)
        weighed = [weigh(g) for g in (2 * q, 2 * q + 1)]
        made = [sides(2 * q + k, *weighed[k], True) for k in range(2)]
        for k in range(2):
            store_eight(rsend, 2 * q + k, made[k])
        send_chunk(2, rsend, rgot, q)

    each_chunk(chunk0, -1)

    for copy in halos0:
        copy.wait_recv()
    clear_edges((cx, mx), ygot)
    lax.fori_loop(0, ROWS, faces, 0)
    (c_ec,) = elastic(cx, ygot, qx, 1, (cx,))
    pick(qx, 1, moves1)
    c_c = jnp.zeros((COLS, DEPTH), F32)
    for c in range(3):
        for i in range(ROWS):
            c_c = c_c + cx[c, i + 1] * cx[c, i + 1]


    def note_targets():
        ids = jnp.concatenate([pgot_ids(g) for g in range(groups)], axis=0)
        target3[...] = jnp.where(ids == lanes3, 1.0, 0.0).astype(BF16)
        targetr[...] = jnp.sum(jnp.where(eye, ids[:, 0:1], 0.0), axis=0, keepdims=True)

    def collect(phase, src, dst):
        batch(phase, src, dst, 0, 0, nb - 1).wait_recv()
        returned = jnp.concatenate([eight(dst, g) for g in range(groups)], axis=0)
        block = fiota((BLOCKS, slots), 0)
        to_own = jnp.where(block == ownr[...], 1.0, 0.0).astype(BF16)
        to_target = jnp.where(block == targetr[...], 1.0, 0.0).astype(BF16)
        rh, rm = parts2(returned)
        sh, sm = parts2(second[...])
        forces[...] = (plain(to_own, rh) + plain(to_own, rm)) + (
            plain(to_target, sh) + plain(to_target, sm)
        )

    def spread(out, base):
        for part in range(2):
            for k in range(BLOCKS):
                at = slice(k * WIDTH, (k + 1) * WIDTH)
                mask = iota((256, WIDTH), 0) == map_ref[0, 0, k : k + 1, :] // DEPTH
                for c in range(3):
                    force = forces[k : k + 1, c * WIDTH : (c + 1) * WIDTH]
                    high = force.astype(BF16).astype(F32)
                    kept = high if part == 0 else force - high
                    lhs[c, part, :, at] = jnp.where(mask, kept, 0.0).astype(BF16)
        cells = jnp.concatenate([ez[k] for k in range(BLOCKS // 2)], axis=1)
        for c in range(3):
            total = lanes_t(lhs[c, 0], cells) + lanes_t(lhs[c, 1], cells)
            out[c, base : base + ROWS] = out[c, base : base + ROWS] + total.reshape(
                ROWS, COLS, DEPTH
            )

    far_count = (nb // near) * na
    place_far = (b // near) * na + a

    def peer_of(stage, other):
        if stage == 0:
            return (base_near + other, a)
        return ((other // na) * near + place_near, lax.rem(other, na))

    def ar_copy(n, stage, peer, slot):
        return pltpu.make_async_remote_copy(
            src_ref=arsend.at[n, stage], dst_ref=argot.at[n, stage, slot],
            send_sem=ar_send.at[n, stage], recv_sem=ar_recv.at[n, stage],
            device_id=peer_of(stage, peer), device_id_type=MESH,
        )

    def ar_start(n, stage, value):
        own, size = ((place_near, near), (place_far, far_count))[stage]
        arsend[n, stage] = value

        def step(t, carry):
            ar_copy(n, stage, wrap(own + t, size), own).start()
            return carry

        lax.fori_loop(1, size, step, 0)
        argot[n, stage, own] = value

    def ar_finish(n, stage):
        own, size = ((place_near, near), (place_far, far_count))[stage]

        for k in range(2):
            at = pl.ds(0, size - 1)
            arrived = pltpu.make_async_remote_copy(
                src_ref=argot.at[n, stage, at], dst_ref=argot.at[n, stage, at],
                send_sem=ar_send.at[n, stage], recv_sem=ar_recv.at[n, stage],
                device_id=peer_of(stage, wrap(own + 1, size)), device_id_type=MESH,
            )
            (arrived.wait_recv, arrived.wait_send)[k]()
        total = argot[n, stage, 0]
        for k in range(1, size):
            total = total + argot[n, stage, k]
        return total

    def rows_of(*sums):
        row = iota((8, WIDTH), 0)
        value = jnp.zeros((8, WIDTH), F32)
        for k, s in enumerate(sums):
            folded = jnp.sum(s, axis=0, keepdims=True)
            folded = sum(
                folded[:, j : j + WIDTH] for j in range(0, folded.shape[1], WIDTH)
            )
            value = jnp.where(row == k, folded, value)
        return value

    def scalar(total, k):
        return jnp.sum(total[k : k + 1], axis=1, keepdims=True)

    note_targets()
    collect(2, rsend, rgot)
    moves1[...] = moves1[...] + forces[...]
    moves_out(3, moves1, fsend, fgot)
    mines[...] = plain(target3[...], mparts[...])
    spread(qx, 1)
    for c in range(3):
        ysend1[0, c] = qx[c, 1 : ROWS + 1, COLS - 1, :]
        ysend1[1, c] = qx[c, 1 : ROWS + 1, 0, :]
    halos1 = [
        halo(6, qx.at[:, last], qx.at[:, 0], (up, a)),
        halo(7, qx.at[:, 1], qx.at[:, last + 1], (down, a)),
        halo(8, ysend1.at[0], ygot1.at[0], (b, right)),
        halo(9, ysend1.at[1], ygot1.at[1], (b, left)),
    ]
    for copy in halos1:
        copy.start()
    ar_start(0, 0, rows_of(c_c, c_ec, moves0[...] * forces[...]))
    def chunk1(q):
        wait_chunk(3, fsend, fgot, q)
        made = []
        for g in (2 * q, 2 * q + 1):
            w = [ws[g * 8 + r] for r in range(8)]
            made.append(sides(g, eight(fgot, g), w, mines[rows8(g)], False))
        for k in range(2):
            store_eight(bsend, 2 * q + k, made[k])
        send_chunk(4, bsend, bgot, q)

    each_chunk(chunk1, -1, 0, chunks // 2)
    ar_start(0, 1, ar_finish(0, 0))
    each_chunk(chunk1, -1, chunks // 2, chunks)
    for copy in halos1:
        copy.wait_recv()
    clear_edges((qx,), ygot1)
    elastic(qx, ygot1, q2, 0, ())


    total0 = ar_finish(0, 1)
    norm0 = scalar(total0, 0)
    step0 = norm0 / (scalar(total0, 1) + scalar(total0, 2))

    def products(i, sums):
        r_r, r_ar = sums
        for c in range(3):
            q = qx[c, i + 1]
            r = cx[c, i + 1] - step0 * q
            r_r = r_r + r * r
            r_ar = r_ar + r * (q - step0 * q2[c, i])
        return r_r, r_ar

    zero = jnp.zeros((COLS, DEPTH), F32)
    r_r, r_ar = lax.fori_loop(0, ROWS, products, (zero, zero))
    collect(4, bsend, bgot)
    r_moves = moves0[...] - step0 * moves1[...]
    ar_start(1, 0, rows_of(r_r, r_ar, -step0 * (r_moves * forces[...])))
    spread(q2, 0)
    ar_start(1, 1, ar_finish(1, 0))
    total1 = ar_finish(1, 1)
    norm1 = scalar(total1, 0)
    product = scalar(total1, 1) + scalar(total1, 2)
    ratio = norm1 / norm0
    step1 = norm1 / (product - ratio * norm1 / step0)
    on_first = step0 + step1 * (1.0 + ratio)
    on_second = step1 * step0


    def finish(i, carry):
        for c in range(3):
            v, q = cx[c, i + 1], qx[c, i + 1]
            disp_ref[c, i] = on_first * v - on_second * q
            res_ref[c, i] = v - on_first * q + on_second * q2[c, i]
        return carry

    lax.fori_loop(0, ROWS, finish, 0)
    for copy in halos0 + halos1:
        copy.wait_send()

    for phase, src, dst in (
        (0, psend, pgot), (2, rsend, rgot), (3, fsend, fgot), (4, bsend, bgot)
    ):
        batch(phase, src, dst, 0, 0, nb - 1).wait_send()


def on_device(nb, na, cotangent, shear, lame, inertia, points, counts, maps, pairs):
    slots = nb * CAP
    grid = (3, ROWS, COLS, DEPTH)
    near = min(16, nb)
    peers = max(near, (nb // near) * na)

    def buffers(width):
        return [pltpu.VMEM((nb, CAP, width), F32)] * 2

    scratch = [
        pltpu.VMEM((3, ROWS + 2, COLS, DEPTH), F32),
        pltpu.VMEM((3, ROWS + 2, COLS, DEPTH), F32),
        pltpu.VMEM(grid, F32),
        pltpu.VMEM((2, ROWS + 2, COLS, DEPTH), F32),
        pltpu.VMEM((ROWS, COLS, DEPTH), F32),
        pltpu.VMEM((6, 2, ROWS, COLS, DEPTH), F32),
        pltpu.VMEM((BLOCKS // 2, DEPTH, 2 * WIDTH), BF16),
        pltpu.VMEM((768, 2 * DEPTH), BF16),
        pltpu.VMEM((3, 2, 256, BLOCKS * WIDTH), BF16),
        pltpu.VMEM((slots, 2 * WIDTH, WIDTH), BF16),
        pltpu.VMEM((BLOCKS, MOVE), F32),
        pltpu.VMEM((BLOCKS, MOVE), F32),
        pltpu.VMEM((WIDTH, MOVE), BF16),
        pltpu.VMEM((WIDTH, MOVE), BF16),
        pltpu.VMEM((slots, WIDTH), BF16),
        pltpu.VMEM((slots, WIDTH), BF16),
        pltpu.VMEM((slots, MOVE), F32),
        pltpu.VMEM((slots, WIDTH), F32),
        pltpu.VMEM((1, slots), F32),
        pltpu.VMEM((1, slots), F32),
        pltpu.VMEM((slots, MOVE), F32),
        pltpu.VMEM((slots, WIDTH), F32),
        pltpu.VMEM((slots, WIDTH), F32),
        pltpu.VMEM((BLOCKS, MOVE), F32),
        *buffers(MOVE + WIDTH + MOVE),
        *buffers(MOVE),
        *buffers(MOVE),
        *buffers(MOVE),
        pltpu.VMEM((2, 5, ROWS, DEPTH), F32),
        pltpu.VMEM((2, 5, ROWS, DEPTH), F32),
        pltpu.VMEM((2, 3, ROWS, DEPTH), F32),
        pltpu.VMEM((2, 3, ROWS, DEPTH), F32),
        pltpu.VMEM((2, 2, 8, WIDTH), F32),
        pltpu.VMEM((2, 2, peers, 8, WIDTH), F32),
        pltpu.SemaphoreType.DMA((4,)),
        pltpu.SemaphoreType.DMA((5,)),
        pltpu.SemaphoreType.DMA((5, nb // 4)),
        pltpu.SemaphoreType.DMA((10,)),
        pltpu.SemaphoreType.DMA((10,)),
        pltpu.SemaphoreType.DMA((2, 2)),
        pltpu.SemaphoreType.DMA((2, 2)),
    ]
    return pl.pallas_call(
        functools.partial(kernel, nb, na),
        out_shape=[pltpu.VMEM(grid, F32)] * 2,
        in_specs=[pl.BlockSpec(memory_space=pl.ANY)] * 4
        + [
            pl.BlockSpec(memory_space=pltpu.VMEM),
            pl.BlockSpec(memory_space=pltpu.SMEM),
            pl.BlockSpec(memory_space=pltpu.VMEM),
            pl.BlockSpec(memory_space=pltpu.VMEM),
        ],
        out_specs=[pl.BlockSpec(memory_space=pltpu.VMEM)] * 2,
        scratch_shapes=scratch,
        compiler_params=pltpu.CompilerParams(
            has_side_effects=True, collective_id=0, vmem_limit_bytes=54 * 2**20
        ),
        name="adjoint_cg",
    )(
        cotangent, shear, lame, inertia,
        points[0, 0].transpose(1, 0, 2), counts, maps, pairs[0].transpose(1, 0, 2),
    )


def solution(mesh):
    nb, na = mesh.shape["body"], mesh.shape["across"]
    split = P("body", "across")
    vector = P(None, "body", "across", None)
    return jax.shard_map(
        functools.partial(on_device, nb, na),
        mesh=mesh,
        in_specs=(vector, split, split, split, split, split, split, split),
        out_specs=(vector, vector),
        check_vma=False,
    )
```

```python
import functools

import jax
import jax.numpy as jnp
from jax import lax
from jax.experimental import pallas as pl
from jax.experimental.pallas import tpu as pltpu
from jax.sharding import PartitionSpec as P

MESH = pl.DeviceIdType.MESH
CAP = 4
ROWS, COLS, DEPTH = 8, 32, 256
BLOCKS, WIDTH = 16, 128
MOVE = 3 * WIDTH
F32, BF16 = jnp.float32, jnp.bfloat16
FAR = 100.0


def iota(shape, dim):
    return lax.broadcasted_iota(jnp.int32, shape, dim)


def fiota(shape, dim):
    return iota(shape, dim).astype(F32)


def parts2(x):
    high = x.astype(BF16)
    return high, (x - high.astype(F32)).astype(BF16)


def parts3(x):
    high = x.astype(BF16).astype(F32)
    rest = x - high
    mid = rest.astype(BF16).astype(F32)
    return high, mid, rest - mid


def lanes_t(a, b):
    return lax.dot_general(a, b, (((1,), (1,)), ((), ())), preferred_element_type=F32)


def plain(a, b):
    return jnp.dot(a, b, preferred_element_type=F32)


def kernel(
    nb, na,
    c_hbm, mu_hbm, lam_hbm, inertia_hbm, pts_ref, cnt_ref, map_ref, pair_ref,
    disp_ref, res_ref,
    cx, qx, q2, mx, inertia, fw, ez, vhm, lhs, ws,
    moves0, moves1, mparts, pparts, own3, target3, mines0, mines, tgtc, ownr, targetr, second, rowt, colt, forces,
    psend, pgot, rsend, rgot, fsend, fgot, bsend, bgot,
    ysend, ygot, ysend1, ygot1, arsend, argot,
    sem_in, a2a_send, a2a_recv, halo_send, halo_recv, ar_send, ar_recv,
):
    b = lax.axis_index("body")
    a = lax.axis_index("across")
    slots = nb * CAP
    groups = nb // 2
    chunks = nb // 4
    me_q = b // 4

    def wrap(i, n):
        return lax.rem(i + n, n)

    near = min(16, nb)
    place_near, base_near = lax.rem(b, near), (b // near) * near
    barrier = pltpu.get_barrier_semaphore()

    def greet(peer):
        pl.semaphore_signal(barrier, inc=1, device_id=peer, device_id_type=MESH)

    def greet_body(t, carry):
        greet((wrap(b + t, nb), a))
        return carry

    lax.fori_loop(1, nb, greet_body, 0)
    for t in range(1, na):
        for k in range(nb // near):
            greet((k * near + place_near, wrap(a + t, na)))

    loads = [
        pltpu.make_async_copy(c_hbm, cx.at[:, pl.ds(1, ROWS)], sem_in.at[0]),
        pltpu.make_async_copy(mu_hbm, mx.at[0, pl.ds(1, ROWS)], sem_in.at[1]),
        pltpu.make_async_copy(lam_hbm, mx.at[1, pl.ds(1, ROWS)], sem_in.at[2]),
        pltpu.make_async_copy(inertia_hbm, inertia, sem_in.at[3]),
    ]
    for load in loads:
        load.start()

    own_row, partner_row, target_row = (pair_ref[k].astype(F32) for k in range(3))
    sub, lane = iota((slots, slots), 0), iota((slots, slots), 1)
    eye = sub == lane
    partner_col = jnp.sum(jnp.where(eye, partner_row, 0.0), axis=1, keepdims=True)
    rank = jnp.sum(
        jnp.where((partner_col == partner_row) & (sub < lane), 1.0, 0.0), axis=0, keepdims=True
    )
    slot_row = partner_row * CAP + rank
    chosen = slot_row == sub.astype(F32)
    own_col = jnp.sum(jnp.where(chosen, own_row, 0.0), axis=1, keepdims=True)
    target_col = jnp.sum(jnp.where(chosen, target_row, 0.0), axis=1, keepdims=True)
    tgtc[...] = jnp.broadcast_to(target_col, (slots, WIDTH))
    ownr[...] = jnp.sum(jnp.where(eye, own_col, 0.0), axis=0, keepdims=True)

    block_id = iota((BLOCKS, WIDTH), 0)
    count = jnp.zeros((BLOCKS, WIDTH), jnp.int32)
    for k in range(BLOCKS):
        count = jnp.where(block_id == k, cnt_ref[0, 0, k], count)
    active = iota((BLOCKS, WIDTH), 1) < count
    far = jnp.where(lax.rem(block_id, 2) == 0, FAR, -FAR)
    coords = [
        jnp.where(active, pts_ref[0] - 0.5, far),
        pts_ref[1] - 0.5,
        pts_ref[2],
    ]
    pad16 = jnp.zeros((BLOCKS, WIDTH), F32)

    def store_parts(ref, tiles):
        for c, tile in enumerate(tiles):
            stacked = jnp.concatenate([*parts3(tile)] + [pad16] * 5, axis=0)
            ref[:, c * WIDTH : (c + 1) * WIDTH] = stacked.astype(BF16)

    store_parts(pparts, coords)
    lane8 = iota((8, WIDTH), 1)
    lane3 = jnp.where(lane8 < 3 * BLOCKS, lax.rem(lane8, BLOCKS), -1).astype(F32)
    sub8 = iota((8, WIDTH), 0)

    lanes = iota((slots, WIDTH), 1)
    lanes3 = jnp.where(lanes < 3 * BLOCKS, lax.rem(lanes, BLOCKS), -1).astype(F32)
    own3[...] = jnp.where(own_col == lanes3, 1.0, 0.0).astype(BF16)

    def select3(ids, ref):
        return plain(jnp.where(ids == lane3, 1.0, 0.0).astype(BF16), ref[...])

    def eight(ref, g):
        return jnp.concatenate([ref[2 * g], ref[2 * g + 1]], axis=0)

    def store_eight(ref, g, value):
        ref[2 * g] = value[:4]
        ref[2 * g + 1] = value[4:]

    def rows8(g):
        return pl.ds(pl.multiple_of(g * 8, 8), 8)

    def a2a(phase, src, dst, peer):
        return pltpu.make_async_remote_copy(
            src_ref=src.at[peer], dst_ref=dst.at[b],
            send_sem=a2a_send.at[phase], recv_sem=a2a_recv.at[phase, arrives(phase, me_q)],
            device_id=(peer, a), device_id_type=MESH,
        )

    def arrives(phase, q):
        return 0 if phase in (2, 4) else q

    def batch(phase, src, dst, q, first, count):
        at = pl.ds(first, count)
        return pltpu.make_async_remote_copy(
            src_ref=src.at[at], dst_ref=dst.at[at],
            send_sem=a2a_send.at[phase], recv_sem=a2a_recv.at[phase, arrives(phase, q)],
            device_id=(wrap(b + 1, nb), a), device_id_type=MESH,
        )

    def send_chunk(phase, src, dst, q):
        @pl.when(q != me_q)
        def _():
            for h in range(4):
                a2a(phase, src, dst, 4 * q + h).start()

        @pl.when(q == me_q)
        def _():
            for h in range(4):
                peer = 4 * q + h

                @pl.when(peer != b)
                def _():
                    a2a(phase, src, dst, peer).start()

                @pl.when(peer == b)
                def _():
                    dst[peer] = src[peer]

    def wait_chunk(phase, src, dst, q):
        @pl.when(q != me_q)
        def _():
            batch(phase, src, dst, q, 4 * q, 4).wait_recv()

        @pl.when(q == me_q)
        def _():
            batch(phase, src, dst, q, 4 * q, 3).wait_recv()

    def each_chunk(body, sign):
        def step(t, carry):
            body(wrap(me_q + sign * t, chunks))
            return carry

        lax.fori_loop(0, chunks, step, 0)

    def store_all(ref, value):
        for k in range(nb):
            ref[k] = value[k * CAP : (k + 1) * CAP]

    def map_row(k):
        pair = map_ref[0, 0, pl.ds(2 * k, 1), :], map_ref[0, 0, pl.ds(2 * k + 1, 1), :]
        return jnp.concatenate(pair, axis=1)

    def place(k, carry):
        z = lax.rem(map_row(k), DEPTH)
        ez[k] = jnp.where(iota((DEPTH, 2 * WIDTH), 0) == z, 1.0, 0.0).astype(BF16)
        return carry

    lax.fori_loop(0, BLOCKS // 2, place, 0)

    def pick(vector, base, moves):
        for c in range(3):
            flat = vector[c, base : base + ROWS].reshape(ROWS * COLS, DEPTH)
            at = slice(c * 256, (c + 1) * 256)
            vhm[at, :DEPTH], vhm[at, DEPTH:] = parts2(flat)

        def step(k, rows):
            picked = plain(vhm[...], jnp.concatenate([ez[k], ez[k]], axis=0))
            mask = iota((256, 2 * WIDTH), 0) == map_row(k) // DEPTH
            made = []
            for c in range(3):
                kept = jnp.where(mask, picked[c * 256 : (c + 1) * 256], 0.0)
                row = jnp.sum(kept, axis=0, keepdims=True)
                lower = jnp.where(block_id == 2 * k, row[:, :WIDTH], rows[c])
                made.append(jnp.where(block_id == 2 * k + 1, row[:, WIDTH:], lower))
            return tuple(made)

        rows = lax.fori_loop(0, BLOCKS // 2, step, (pad16,) * 3)
        moves[...] = jnp.concatenate(rows, axis=1)

    for load in loads:
        load.wait()
    pick(cx, 1, moves0)

    def tiles(value):
        return [value[:, c * WIDTH : (c + 1) * WIDTH] for c in range(3)]

    def moves_out(phase, moves, src, dst):
        store_parts(mparts, tiles(moves[...]))

        store_all(src, plain(own3[...], mparts[...]))
        each_chunk(lambda q: send_chunk(phase, src, dst, q), 1)

    store_parts(mparts, tiles(moves0[...]))
    first = [plain(own3[...], pparts[...]), tgtc[...], plain(own3[...], mparts[...])]
    store_all(psend, jnp.concatenate(first, axis=1))

    up, down = wrap(b + 1, nb), wrap(b - 1, nb)
    right, left = wrap(a + 1, na), wrap(a - 1, na)

    def halo(k, src, dst, peer):
        return pltpu.make_async_remote_copy(
            src_ref=src, dst_ref=dst, send_sem=halo_send.at[k], recv_sem=halo_recv.at[k],
            device_id=peer, device_id_type=MESH,
        )

    last = ROWS
    for c in range(3):
        ysend[0, c] = cx[c, 1 : ROWS + 1, COLS - 1, :]
        ysend[1, c] = cx[c, 1 : ROWS + 1, 0, :]
    for m in range(2):
        ysend[0, 3 + m] = mx[m, 1 : ROWS + 1, COLS - 1, :]
        ysend[1, 3 + m] = mx[m, 1 : ROWS + 1, 0, :]
    halos0 = [
        halo(0, cx.at[:, last], cx.at[:, 0], (up, a)),
        halo(1, cx.at[:, 1], cx.at[:, last + 1], (down, a)),
        halo(2, mx.at[:, last], mx.at[:, 0], (up, a)),
        halo(3, mx.at[:, 1], mx.at[:, last + 1], (down, a)),
        halo(4, ysend.at[0], ygot.at[0], (b, right)),
        halo(5, ysend.at[1], ygot.at[1], (b, left)),
    ]
    pl.semaphore_wait(barrier, nb - 1 + (na - 1) * (nb // near))
    each_chunk(lambda q: send_chunk(0, psend, pgot, q), 1)
    for copy in halos0:
        copy.start()

    row32, lane256 = iota((COLS, DEPTH), 0), iota((COLS, DEPTH), 1)

    def clear_edges(xs, yhalo):
        @pl.when(b == 0)
        def _():
            for x in xs:
                x[:, 0] = jnp.zeros_like(x[:, 0])

        @pl.when(b == nb - 1)
        def _():
            for x in xs:
                x[:, last + 1] = jnp.zeros_like(x[:, last + 1])

        @pl.when(a == 0)
        def _():
            yhalo[0] = jnp.zeros_like(yhalo[0])

        @pl.when(a == na - 1)
        def _():
            yhalo[1] = jnp.zeros_like(yhalo[1])

    def beside(v, low, high):
        return (
            jnp.where(row32 == COLS - 1, high, pltpu.roll(v, COLS - 1, 0)),
            jnp.where(row32 == 0, low, pltpu.roll(v, 1, 0)),
            jnp.where(lane256 == DEPTH - 1, 0.0, pltpu.roll(v, DEPTH - 1, 1)),
            jnp.where(lane256 == 0, 0.0, pltpu.roll(v, 1, 1)),
        )

    def faces(i, carry):
        mu, lam = mx[0, i + 1], mx[1, i + 1]
        near_mu = (mx[0, i + 2], mx[0, i]) + beside(
            mu, ygot[0, 3, pl.ds(i, 1), :], ygot[1, 3, pl.ds(i, 1), :]
        )
        near_lam = (mx[1, i + 2], mx[1, i]) + beside(
            lam, ygot[0, 4, pl.ds(i, 1), :], ygot[1, 4, pl.ds(i, 1), :]
        )
        cut = nb // 4
        open_high = jnp.where((b == cut - 1) & (i == ROWS - 1), 0.0, 0.5)
        open_low = jnp.where((b == cut) & (i == 0), 0.0, 0.5)
        for k in range(6):
            half = (open_high, open_low, 0.5, 0.5, 0.5, 0.5)[k]
            plain_weight = half * (mu + near_mu[k])
            fw[k, 0, i] = plain_weight
            fw[k, 1, i] = 2.0 * plain_weight + half * (lam + near_lam[k])
        return carry

    def elastic(vector, yhalo, out, base, others):
        def plane(i, sums):
            sums = list(sums)
            for c in range(3):
                v = vector[c, i + 1]
                near = (vector[c, i + 2], vector[c, i]) + beside(
                    v, yhalo[0, c, pl.ds(i, 1), :], yhalo[1, c, pl.ds(i, 1), :]
                )
                value = inertia[i] * v
                for k in range(6):
                    value = value + fw[k, int(k // 2 == c), i] * (v - near[k])
                out[c, base + i] = value
                for n, other in enumerate(others):
                    sums[n] = sums[n] + value * other[c, i + 1]
            return tuple(sums)

        zero = jnp.zeros((COLS, DEPTH), F32)
        return lax.fori_loop(0, ROWS, plane, (zero,) * len(others))

    ones8 = jnp.ones((8, WIDTH), F32)

    def weigh(g):
        got = eight(pgot, g)
        ids = got[:, MOVE : MOVE + WIDTH]
        picked = jnp.where(ids == lane3, 1.0, 0.0).astype(BF16)
        picked = plain(picked, jnp.concatenate([pparts[...], mparts[...]], axis=1))
        ys, mine = tiles(picked), picked[:, MOVE:]
        made = []
        pad = jnp.zeros((WIDTH - 24, WIDTH), F32)
        xs = jnp.concatenate(tiles(got) + [pad], axis=0).T
        for r in range(8):
            squared = None
            for c in range(3):
                apart = xs[:, 8 * c + r : 8 * c + r + 1] - ys[c][r : r + 1]
                squared = apart * apart if squared is None else squared + apart * apart
            squared = jnp.minimum(squared, 1.0)
            inverse = 1.0 / squared
            weight = 0.005 * (inverse * (inverse + 2.0) - 3.0) - 0.01 * jnp.log(squared)
            made.append(jnp.concatenate(parts2(weight), axis=0))
            ws[g * 8 + r] = made[r]
        return got[:, MOVE + WIDTH :], made, mine

    def halves(value, extra):
        rows = []
        for tile in tiles(value):
            high = tile.astype(BF16).astype(F32)
            rows += [high, tile - high]
        return rows + extra

    def only(rows, keep):
        kept = [jnp.where(keep, row, 0.0) for row in rows]
        return jnp.concatenate(kept, axis=0).astype(BF16)

    def sides(g, got, w, mine, first_phase):
        extra = [ones8, ones8] if first_phase else []
        v_rows, u_rows = halves(got, extra), halves(mine, extra)
        v_side, w_side = [], []
        for q in range(4):
            kept = only(v_rows, lax.rem(sub8, 4) == q)
            v_side += [kept, kept]
            w_side.append(jnp.concatenate([w[q], w[q + 4]], axis=1))
        to_second = plain(jnp.concatenate(v_side, axis=1), jnp.concatenate(w_side, axis=0))
        u_side = jnp.concatenate([only(u_rows, sub8 == r) for r in range(8)], axis=1)
        to_first = lanes_t(u_side, jnp.concatenate(w, axis=1))
        to_first = to_first[:, :WIDTH] + to_first[:, WIDTH:]
        into_second, into_first = [], []
        for k in range(len(v_rows)):
            at = slice(8 * k, 8 * k + 8)
            into_second.append(
                jnp.where(sub8 < 4, to_second[at, :WIDTH], to_second[at, WIDTH:])
            )
            into_first.append(to_first[at])
        at = rows8(g)
        if first_phase:
            rowt[at], colt[at] = into_first[6], into_second[6]
        row_total, col_total = rowt[at], colt[at]

        def force(move, total, parts, c):
            return move * total - (parts[2 * c] + parts[2 * c + 1])

        to_keep = jnp.concatenate(
            [force(u, col_total, into_second, c) for c, u in enumerate(tiles(mine))], axis=1
        )
        second[at] = to_keep
        to_return = jnp.concatenate(
            [force(v, row_total, into_first, c) for c, v in enumerate(tiles(got))], axis=1
        )
        return to_return, to_keep

    def pgot_ids(g):
        return jnp.concatenate([pgot[2 * g, :, MOVE : MOVE + WIDTH], pgot[2 * g + 1, :, MOVE : MOVE + WIDTH]], axis=0)

    def chunk0(q):
        wait_chunk(0, psend, pgot, q)
        weighed = [weigh(g) for g in (2 * q, 2 * q + 1)]
        made = [sides(2 * q + k, *weighed[k], True) for k in range(2)]
        for k in range(2):
            store_eight(rsend, 2 * q + k, made[k][0])
            mines0[rows8(2 * q + k)] = weighed[k][2]
        send_chunk(2, rsend, rgot, q)

    c_c = jnp.zeros((1, DEPTH), F32)
    for c in range(3):
        for i in range(ROWS):
            square = cx[c, i + 1] * cx[c, i + 1]
            c_c = c_c + jnp.sum(square, axis=0, keepdims=True)
    each_chunk(chunk0, -1)

    for copy in halos0:
        copy.wait_recv()
    clear_edges((cx, mx), ygot)
    lax.fori_loop(0, ROWS, faces, 0)
    (c_ec,) = elastic(cx, ygot, qx, 1, (cx,))
    pick(qx, 1, moves1)


    def note_targets():
        ids = jnp.concatenate([pgot_ids(g) for g in range(groups)], axis=0)
        target3[...] = jnp.where(ids == lanes3, 1.0, 0.0).astype(BF16)
        targetr[...] = jnp.sum(jnp.where(eye, ids[:, 0:1], 0.0), axis=0, keepdims=True)

    def collect(phase, src, dst):
        batch(phase, src, dst, 0, 0, nb - 1).wait_recv()
        returned = jnp.concatenate([eight(dst, g) for g in range(groups)], axis=0)
        block = fiota((BLOCKS, slots), 0)
        to_own = jnp.where(block == ownr[...], 1.0, 0.0).astype(BF16)
        to_target = jnp.where(block == targetr[...], 1.0, 0.0).astype(BF16)
        rh, rm = parts2(returned)
        sh, sm = parts2(second[...])
        forces[...] = (plain(to_own, rh) + plain(to_own, rm)) + (
            plain(to_target, sh) + plain(to_target, sm)
        )

    def spread(out, base):
        for part in range(2):
            for k in range(BLOCKS):
                at = slice(k * WIDTH, (k + 1) * WIDTH)
                mask = iota((256, WIDTH), 0) == map_ref[0, 0, k : k + 1, :] // DEPTH
                for c in range(3):
                    force = forces[k : k + 1, c * WIDTH : (c + 1) * WIDTH]
                    high = force.astype(BF16).astype(F32)
                    kept = high if part == 0 else force - high
                    lhs[c, part, :, at] = jnp.where(mask, kept, 0.0).astype(BF16)
        cells = jnp.concatenate([ez[k] for k in range(BLOCKS // 2)], axis=1)
        for c in range(3):
            total = lanes_t(lhs[c, 0], cells) + lanes_t(lhs[c, 1], cells)
            out[c, base : base + ROWS] = out[c, base : base + ROWS] + total.reshape(
                ROWS, COLS, DEPTH
            )

    far_count = (nb // near) * na
    place_far = (b // near) * na + a

    def peer_of(stage, other):
        if stage == 0:
            return (base_near + other, a)
        return ((other // na) * near + place_near, lax.rem(other, na))

    def ar_copy(n, stage, peer, slot):
        return pltpu.make_async_remote_copy(
            src_ref=arsend.at[n, stage], dst_ref=argot.at[n, stage, slot],
            send_sem=ar_send.at[n, stage], recv_sem=ar_recv.at[n, stage],
            device_id=peer_of(stage, peer), device_id_type=MESH,
        )

    def ar_start(n, stage, value):
        own, size = ((place_near, near), (place_far, far_count))[stage]
        arsend[n, stage] = value

        def step(t, carry):
            ar_copy(n, stage, wrap(own + t, size), own).start()
            return carry

        lax.fori_loop(1, size, step, 0)
        argot[n, stage, own] = value

    def ar_finish(n, stage):
        own, size = ((place_near, near), (place_far, far_count))[stage]

        for k in range(2):
            at = pl.ds(0, size - 1)
            arrived = pltpu.make_async_remote_copy(
                src_ref=argot.at[n, stage, at], dst_ref=argot.at[n, stage, at],
                send_sem=ar_send.at[n, stage], recv_sem=ar_recv.at[n, stage],
                device_id=peer_of(stage, wrap(own + 1, size)), device_id_type=MESH,
            )
            (arrived.wait_recv, arrived.wait_send)[k]()
        total = argot[n, stage, 0]
        for k in range(1, size):
            total = total + argot[n, stage, k]
        return total

    def rows_of(*sums):
        row = iota((8, WIDTH), 0)
        value = jnp.zeros((8, WIDTH), F32)
        for k, s in enumerate(sums):
            folded = jnp.sum(s, axis=0, keepdims=True)
            folded = sum(
                folded[:, j : j + WIDTH] for j in range(0, folded.shape[1], WIDTH)
            )
            value = jnp.where(row == k, folded, value)
        return value

    def scalar(total, k):
        return jnp.sum(total[k : k + 1], axis=1, keepdims=True)

    note_targets()
    collect(2, rsend, rgot)
    moves1[...] = moves1[...] + forces[...]
    moves_out(3, moves1, fsend, fgot)
    mines[...] = plain(target3[...], mparts[...])
    spread(qx, 1)
    for c in range(3):
        ysend1[0, c] = qx[c, 1 : ROWS + 1, COLS - 1, :]
        ysend1[1, c] = qx[c, 1 : ROWS + 1, 0, :]
    halos1 = [
        halo(6, qx.at[:, last], qx.at[:, 0], (up, a)),
        halo(7, qx.at[:, 1], qx.at[:, last + 1], (down, a)),
        halo(8, ysend1.at[0], ygot1.at[0], (b, right)),
        halo(9, ysend1.at[1], ygot1.at[1], (b, left)),
    ]
    for copy in halos1:
        copy.start()
    ar_start(0, 0, rows_of(c_c, c_ec, moves0[...] * forces[...]))
    together = 2 if chunks % 4 == 0 else 1

    def fold(value):
        return sum(tiles(value))

    def chunks1(t, sums):
        with_c, with_q = sums
        here = [wrap(me_q - together * t - k, chunks) for k in range(together)]
        for q in here:
            wait_chunk(3, fsend, fgot, q)
        made = []
        for g in [2 * q + k for q in here for k in range(2)]:
            w = [ws[g * 8 + r] for r in range(8)]
            got, mine = eight(fgot, g), mines[rows8(g)]
            to_return, to_keep = sides(g, got, w, mine, False)
            got0, mine0 = eight(pgot, g)[:, MOVE + WIDTH :], mines0[rows8(g)]
            with_c = with_c + fold(got0 * to_return + mine0 * to_keep)
            with_q = with_q + fold(got * to_return + mine * to_keep)
            made.append((g, to_return))
        for g, value in made:
            store_eight(bsend, g, value)
        for q in here:
            send_chunk(4, bsend, bgot, q)
        return with_c, with_q

    steps = chunks // together
    sums = (jnp.zeros((8, WIDTH), F32),) * 2
    sums = lax.fori_loop(0, steps // 2, chunks1, sums)
    ar_start(0, 1, ar_finish(0, 0))
    contact_c, contact_q = lax.fori_loop(steps // 2, steps, chunks1, sums)
    for copy in halos1:
        copy.wait_recv()
    clear_edges((qx,), ygot1)
    elastic(qx, ygot1, q2, 0, ())


    total0 = ar_finish(0, 1)
    norm0 = scalar(total0, 0)
    step0 = norm0 / (scalar(total0, 1) + scalar(total0, 2))

    def products(i, sums):
        r_r, r_ar = sums
        for c in range(3):
            q = qx[c, i + 1]
            r = cx[c, i + 1] - step0 * q
            r_r = r_r + r * r
            r_ar = r_ar + r * (q - step0 * q2[c, i])
        return r_r, r_ar

    zero = jnp.zeros((COLS, DEPTH), F32)
    r_r, r_ar = lax.fori_loop(0, ROWS, products, (zero, zero))
    ar_start(1, 0, rows_of(r_r, r_ar, -step0 * (contact_c - step0 * contact_q)))
    collect(4, bsend, bgot)
    ar_start(1, 1, ar_finish(1, 0))
    spread(q2, 0)
    total1 = ar_finish(1, 1)
    norm1 = scalar(total1, 0)
    product = scalar(total1, 1) + scalar(total1, 2)
    ratio = norm1 / norm0
    step1 = norm1 / (product - ratio * norm1 / step0)
    on_first = step0 + step1 * (1.0 + ratio)
    on_second = step1 * step0


    def finish(i, carry):
        for c in range(3):
            v, q = cx[c, i + 1], qx[c, i + 1]
            disp_ref[c, i] = on_first * v - on_second * q
            res_ref[c, i] = v - on_first * q + on_second * q2[c, i]
        return carry

    lax.fori_loop(0, ROWS, finish, 0)
    for copy in halos0 + halos1:
        copy.wait_send()

    for phase, src, dst in (
        (0, psend, pgot), (2, rsend, rgot), (3, fsend, fgot), (4, bsend, bgot)
    ):
        batch(phase, src, dst, 0, 0, nb - 1).wait_send()


def on_device(nb, na, cotangent, shear, lame, inertia, points, counts, maps, pairs):
    slots = nb * CAP
    grid = (3, ROWS, COLS, DEPTH)
    near = min(16, nb)
    peers = max(near, (nb // near) * na)

    def buffers(width):
        return [pltpu.VMEM((nb, CAP, width), F32)] * 2

    scratch = [
        pltpu.VMEM((3, ROWS + 2, COLS, DEPTH), F32),
        pltpu.VMEM((3, ROWS + 2, COLS, DEPTH), F32),
        pltpu.VMEM(grid, F32),
        pltpu.VMEM((2, ROWS + 2, COLS, DEPTH), F32),
        pltpu.VMEM((ROWS, COLS, DEPTH), F32),
        pltpu.VMEM((6, 2, ROWS, COLS, DEPTH), F32),
        pltpu.VMEM((BLOCKS // 2, DEPTH, 2 * WIDTH), BF16),
        pltpu.VMEM((768, 2 * DEPTH), BF16),
        pltpu.VMEM((3, 2, 256, BLOCKS * WIDTH), BF16),
        pltpu.VMEM((slots, 2 * WIDTH, WIDTH), BF16),
        pltpu.VMEM((BLOCKS, MOVE), F32),
        pltpu.VMEM((BLOCKS, MOVE), F32),
        pltpu.VMEM((WIDTH, MOVE), BF16),
        pltpu.VMEM((WIDTH, MOVE), BF16),
        pltpu.VMEM((slots, WIDTH), BF16),
        pltpu.VMEM((slots, WIDTH), BF16),
        pltpu.VMEM((slots, MOVE), F32),
        pltpu.VMEM((slots, MOVE), F32),
        pltpu.VMEM((slots, WIDTH), F32),
        pltpu.VMEM((1, slots), F32),
        pltpu.VMEM((1, slots), F32),
        pltpu.VMEM((slots, MOVE), F32),
        pltpu.VMEM((slots, WIDTH), F32),
        pltpu.VMEM((slots, WIDTH), F32),
        pltpu.VMEM((BLOCKS, MOVE), F32),
        *buffers(MOVE + WIDTH + MOVE),
        *buffers(MOVE),
        *buffers(MOVE),
        *buffers(MOVE),
        pltpu.VMEM((2, 5, ROWS, DEPTH), F32),
        pltpu.VMEM((2, 5, ROWS, DEPTH), F32),
        pltpu.VMEM((2, 3, ROWS, DEPTH), F32),
        pltpu.VMEM((2, 3, ROWS, DEPTH), F32),
        pltpu.VMEM((2, 2, 8, WIDTH), F32),
        pltpu.VMEM((2, 2, peers, 8, WIDTH), F32),
        pltpu.SemaphoreType.DMA((4,)),
        pltpu.SemaphoreType.DMA((5,)),
        pltpu.SemaphoreType.DMA((5, nb // 4)),
        pltpu.SemaphoreType.DMA((10,)),
        pltpu.SemaphoreType.DMA((10,)),
        pltpu.SemaphoreType.DMA((2, 2)),
        pltpu.SemaphoreType.DMA((2, 2)),
    ]
    return pl.pallas_call(
        functools.partial(kernel, nb, na),
        out_shape=[pltpu.VMEM(grid, F32)] * 2,
        in_specs=[pl.BlockSpec(memory_space=pl.ANY)] * 4
        + [
            pl.BlockSpec(memory_space=pltpu.VMEM),
            pl.BlockSpec(memory_space=pltpu.SMEM),
            pl.BlockSpec(memory_space=pltpu.VMEM),
            pl.BlockSpec(memory_space=pltpu.VMEM),
        ],
        out_specs=[pl.BlockSpec(memory_space=pltpu.VMEM)] * 2,
        scratch_shapes=scratch,
        compiler_params=pltpu.CompilerParams(
            has_side_effects=True, collective_id=0, vmem_limit_bytes=54 * 2**20
        ),
        name="adjoint_cg",
    )(
        cotangent, shear, lame, inertia,
        points[0, 0].transpose(1, 0, 2), counts, maps, pairs[0].transpose(1, 0, 2),
    )


def solution(mesh):
    nb, na = mesh.shape["body"], mesh.shape["across"]
    split = P("body", "across")
    vector = P(None, "body", "across", None)
    return jax.shard_map(
        functools.partial(on_device, nb, na),
        mesh=mesh,
        in_specs=(vector, split, split, split, split, split, split, split),
        out_specs=(vector, vector),
        check_vma=False,
    )
```
